32 devices in a mesh: wide: 16 (over z, y, x), narrow: 2 (over core).
Axes of the slice: x: 2, y: 2, z: 4, core: 2. Of those that a mesh axis runs over, the one named last changes fastest.
Arguments:
- patches: bfloat16 [16384, 768], P(('wide', 'narrow')), may hold values from -6 to 6
- pieces: int32 [16, 12], P('wide'), may hold values from 1 to 196, 1024 in all within a row
- ln1_gain: float32 [768], replicated, may hold values from 0.25 to 1.75
- ln1_bias: float32 [768], replicated, may hold values from -1.8 to 1.8
- qkv_weight: bfloat16 [3, 768, 768], P(None, None, 'narrow'), may hold values from -0.21875 to 0.21875
- qkv_bias: float32 [2, 768], P(None, 'narrow'), may hold values from -1.8 to 1.8
- out_weight: bfloat16 [768, 768], P('narrow'), may hold values from -0.875 to 0.875
- out_bias: float32 [768], replicated, may hold values from -1.8 to 1.8
- attn_scale: float32 [768], replicated, may hold values from 0.25 to 1.75
- ln2_gain: float32 [768], replicated, may hold values from 0.25 to 1.75
- ln2_bias: float32 [768], replicated, may hold values from -1.8 to 1.8
- fc1_weight: bfloat16 [768, 3072], P(None, 'narrow'), may hold values from -0.21875 to 0.21875
- fc1_bias: float32 [3072], P('narrow'), may hold values from -1.8 to 1.8
- fc2_weight: bfloat16 [3072, 768], P('narrow'), may hold values from -0.21875 to 0.21875
- fc2_bias: float32 [768], replicated, may hold values from -1.8 to 1.8
- mlp_scale: float32 [768], replicated, may hold values from 0.25 to 1.75
- cotangent: bfloat16 [16384, 768], P(('wide', 'narrow')), may hold values from -6 to 6
Outputs:
- output: bfloat16 [16384, 768], P(('wide', 'narrow'))
- grad_patches: float32 [16384, 768], P(('wide', 'narrow'))
- grad_ln1_gain: float32 [768], replicated
- grad_ln1_bias: float32 [768], replicated
- grad_qkv_weight: float32 [3, 768, 768], P(None, None, 'narrow')
- grad_qkv_bias: float32 [2, 768], P(None, 'narrow')
- grad_out_weight: float32 [768, 768], P('narrow')
- grad_out_bias: float32 [768], replicated
- grad_attn_scale: float32 [768], replicated
- grad_ln2_gain: float32 [768], replicated
- grad_ln2_bias: float32 [768], replicated
- grad_fc1_weight: float32 [768, 3072], P(None, 'narrow')
- grad_fc1_bias: float32 [3072], P('narrow')
- grad_fc2_weight: float32 [3072, 768], P('narrow')
- grad_fc2_bias: float32 [768], replicated
- grad_mlp_scale: float32 [768], replicated
The draws below stay inside these ranges and needn't reach their ends.
Inputs may be any that keep to these rules, and one draw needn't show every extreme that they name: `pieces`: row s holds the visible-patch counts of the 11 images packed in order into sequence s, then the count of padding positions at its end; each row sums to 1024.
All inputs are finite; a program needn't handle non-finite values.
Results may differ from the reference program's by a relative error of at most 0.017.
Values may be sent and summed in bfloat16 or wider, within the bound.
No kernel may reach another device: no remote copies, remote signals or barrier semaphores. Data moves between devices by JAX's collectives and lax.ppermute only.
A program may use at most 192 MiB of HBM per device.

```python
import math
import jax
import jax.numpy as jnp
import numpy as np
from jax import lax

D = 768
HEADS = 12
HEAD = 64
FF = 3072
SEQ_LEN = 1024
IMGS = 11
MOST_IMG = 196
SEQS = 16
TOKENS = 16384


def block_levels(key, dims, split, low, high):
    level, own = 1.0, jax.random.fold_in(key, 6)
    for position, shards_of in split:
        steps = jnp.exp(jax.random.uniform(jax.random.fold_in(own, position), (shards_of,), jnp.float32, low / len(split), high / len(split)))
        level = level * jnp.repeat(steps, dims[position] // shards_of).reshape([-1 if axis == position else 1 for axis in range(len(dims))])
    return level


def split_up(count, total, limit, skew):
    portions = [(1 << 20) // math.isqrt(rank ** skew) + 1 for rank in range(2, count + 1)]
    surplus, given = total - limit - (count - 1), [1] * (count - 1)
    while surplus > 0:
        free = [i for i in range(count - 1) if given[i] < limit]
        whole, budget = sum([portions[i] for i in free]), surplus
        for i in free:
            addition = min(limit - given[i], max(1, budget * portions[i] // whole), surplus)
            given[i] = given[i] + addition
            surplus = surplus - addition
    return np.array([limit] + given)


def uneven_parts(stream_key, number_of, total, bound, slope):
    if number_of == 2:
        one = jax.random.randint(stream_key, (), max(1, total - bound), min(bound, total - 1) + 1)
        return jnp.stack([one, total - one])
    lengths = jnp.asarray(split_up(number_of, total, bound, slope), jnp.int32)
    twos = (number_of - 1) // 2
    donor, taker = lengths[1:1 + 2 * twos:2], lengths[2:2 + 2 * twos:2]
    room = jnp.minimum(donor - 1, bound - taker)
    passed = jax.random.randint(jax.random.fold_in(stream_key, 1), (twos,), 0, 1 << 20) % (room + 1)
    lengths = lengths.at[1:1 + 2 * twos:2].set(donor - passed).at[2:2 + 2 * twos:2].set(taker + passed)
    return lengths[jax.random.permutation(jax.random.fold_in(stream_key, 2), number_of)]


def bell_draw(stream_key, shape, scale, bound, split=(), held_as=jnp.bfloat16):
    loudness = block_levels(stream_key, shape, split, -0.22, 0.18) if split else 1.0
    entries = jax.random.normal(stream_key, shape, jnp.float32) * scale * loudness
    return jnp.minimum(jnp.maximum(entries, -bound), bound).astype(held_as)


def setup_inputs(seed: int = 0) -> dict:
    streams_of = jax.random.split(jax.random.key(seed), 18)
    return {
        "patches": bell_draw(streams_of[0], (TOKENS, D), 1.0, 6.0, ((0, 32),)),
        "pieces": jax.vmap(lambda own: uneven_parts(own, IMGS + 1, SEQ_LEN, MOST_IMG, 2))(jax.random.split(streams_of[1], SEQS)).reshape((SEQS, IMGS + 1)).astype(jnp.int32),
        "ln1_gain": jnp.clip(1.0 + 0.15 * jax.random.normal(streams_of[2], (D,), jnp.float32), 0.25, 1.75),
        "ln1_bias": bell_draw(streams_of[3], (D,), 0.3, 1.8, (), jnp.float32),
        "qkv_weight": bell_draw(streams_of[4], (3, D, D), D ** -0.5, 0.21875, ((2, 2),)),
        "qkv_bias": bell_draw(streams_of[5], (2, D), 0.3, 1.8, ((1, 2),), jnp.float32),
        "out_weight": bell_draw(streams_of[6], (D, D), (D // 16) ** -0.5, 0.875, ((0, 2),)),
        "out_bias": bell_draw(streams_of[7], (D,), 0.3, 1.8, (), jnp.float32),
        "attn_scale": jnp.clip(1.0 + 0.15 * jax.random.normal(streams_of[8], (D,), jnp.float32), 0.25, 1.75),
        "ln2_gain": jnp.clip(1.0 + 0.15 * jax.random.normal(streams_of[9], (D,), jnp.float32), 0.25, 1.75),
        "ln2_bias": bell_draw(streams_of[10], (D,), 0.3, 1.8, (), jnp.float32),
        "fc1_weight": bell_draw(streams_of[11], (D, FF), D ** -0.5, 0.21875, ((1, 2),)),
        "fc1_bias": bell_draw(streams_of[12], (FF,), 0.3, 1.8, ((0, 2),), jnp.float32),
        "fc2_weight": bell_draw(streams_of[13], (FF, D), (FF // 4) ** -0.5, 0.21875, ((0, 2),)),
        "fc2_bias": bell_draw(streams_of[14], (D,), 0.3, 1.8, (), jnp.float32),
        "mlp_scale": jnp.clip(1.0 + 0.15 * jax.random.normal(streams_of[15], (D,), jnp.float32), 0.25, 1.75),
        "cotangent": bell_draw(streams_of[16], (TOKENS, D), 1.0, 6.0, ((0, 32),)),
    }


@jax.custom_vjp
def low(v):
    return lax.optimization_barrier(v.astype(jnp.bfloat16)).astype(jnp.float32)

@jax.custom_vjp
def low_back(v):
    return v

def low_keep(v):
    return (low(v), None)

def low_pass(kept, grad):
    return (grad,)

def back_keep(v):
    return (v, None)

def back_low(kept, grad):
    return (low(grad),)
low.defvjp(low_keep, low_pass)
low_back.defvjp(back_keep, back_low)
epsilon = 1e-06
masked_score = -1e+30
highest = lax.Precision.HIGHEST

def normalize(values, gain_vec, bias_vec):
    average = lax.optimization_barrier(jnp.mean(values, axis=-1, keepdims=True))
    centred = values - average
    inverse = lax.rsqrt(lax.optimization_barrier(jnp.mean(centred * centred, axis=-1, keepdims=True)) + epsilon)
    return centred * inverse * gain_vec + bias_vec

def segment_ids(pieces, length):
    boundary = jnp.cumsum(pieces, axis=1)[:, :-1]
    places = jnp.arange(length, dtype=jnp.int32)
    return lax.optimization_barrier(jnp.sum((places[None, :, None] >= boundary[:, None, :]).astype(jnp.int32), axis=2))

def attend(operands):
    queries, key_rows, value_rows, segment = operands
    places = jnp.arange(SEQ_LEN, dtype=jnp.int32)
    same_image = (segment[:, None] == segment[None, :]) & (segment[None, :] < IMGS)
    allowed = same_image | (places[:, None] == places[None, :])
    scores = jnp.einsum('qhe,khe->hqk', queries, key_rows, precision=highest) * (1.0 / math.sqrt(HEAD))
    scores = low_back(scores)
    scores = jnp.where(allowed[None], scores, masked_score)
    shares = low(jax.nn.softmax(scores, axis=-1))
    return jnp.einsum('hqk,khe->qhe', shares, value_rows, precision=highest)

def reference(patches, pieces, ln1_gain, ln1_bias, qkv_weight, qkv_bias, out_weight, out_bias, attn_scale, ln2_gain, ln2_bias, fc1_weight, fc1_bias, fc2_weight, fc2_bias, mlp_scale, cotangent):
    segment = segment_ids(pieces, SEQ_LEN)

    def encoder_layer(inputs, ln1_gain, ln1_bias, qkv_weight, qkv_bias, out_weight, out_bias, attn_scale, ln2_gain, ln2_bias, fc1_weight, fc1_bias, fc2_weight, fc2_bias, mlp_scale):
        normed1 = low(normalize(inputs, ln1_gain, ln1_bias))
        bias_rows = jnp.stack([qkv_bias[0], jnp.zeros_like(qkv_bias[0]), qkv_bias[1]])
        mixed = jnp.einsum('td,cde->tce', normed1, qkv_weight, precision=highest) + bias_rows
        mixed = low(low_back(mixed)).reshape(SEQS, SEQ_LEN, 3, HEADS, HEAD)
        attended = lax.map(jax.checkpoint(attend), (mixed[:, :, 0], mixed[:, :, 1], mixed[:, :, 2], segment))
        attended = low(low_back(attended.reshape(TOKENS, D)))
        attn_proj = low_back(jnp.dot(attended, out_weight, precision=highest) + out_bias)
        middle = inputs + attn_scale * attn_proj
        normed2 = low(normalize(middle, ln2_gain, ln2_bias))
        before = low_back(jnp.dot(normed2, fc1_weight, precision=highest) + fc1_bias)
        hidden = low(jax.nn.gelu(before, approximate=False))
        mlp_out = low_back(jnp.dot(hidden, fc2_weight, precision=highest) + fc2_bias)
        return middle + mlp_scale * mlp_out
    floats = [entry.astype(jnp.float32) for entry in (patches, ln1_gain, ln1_bias, qkv_weight, qkv_bias, out_weight, out_bias, attn_scale, ln2_gain, ln2_bias, fc1_weight, fc1_bias, fc2_weight, fc2_bias, mlp_scale)]
    result, pullback = jax.vjp(encoder_layer, *floats)
    gradients = pullback(cotangent.astype(jnp.float32))
    return (result.astype(jnp.bfloat16), gradients[0], gradients[1], gradients[2], gradients[3], gradients[4], gradients[5], gradients[6], gradients[7], gradients[8], gradients[9], gradients[10], gradients[11], gradients[12], gradients[13], gradients[14])
```

```python
from functools import partial
import math

import jax
import jax.numpy as jnp
from jax import lax
from jax.sharding import PartitionSpec as P
from jax.experimental import pallas as pl
from jax.experimental.pallas import tpu as pltpu

HEAD = 64
PAIR = 2 * HEAD
HALO = 256
BLOCK = 128

epsilon = 1e-06
masked_score = -1e30

bf16 = jnp.bfloat16
f32 = jnp.float32

WHOLE = pl.BlockSpec(memory_space=pltpu.VMEM)
SCALARS = pl.BlockSpec(memory_space=pltpu.SMEM)


def params(mib=56):
    return pltpu.CompilerParams(vmem_limit_bytes=mib * 1024 * 1024)


def cost(flops, nbytes, transcendentals=0):
    return pl.CostEstimate(
        flops=int(flops), bytes_accessed=int(nbytes), transcendentals=int(transcendentals)
    )


def shape(dims, dtype):
    return jax.ShapeDtypeStruct(dims, dtype)


def dot(a, b):
    return jnp.dot(a, b, preferred_element_type=f32)


def dot_bt(a, b):
    return lax.dot_general(a, b, (((1,), (1,)), ((), ())), preferred_element_type=f32)


def dot_at(a, b):
    return lax.dot_general(a, b, (((0,), (0,)), ((), ())), preferred_element_type=f32)


def row_stats(values):
    average = jnp.mean(values, axis=-1, keepdims=True)
    centred = values - average
    inverse = lax.rsqrt(jnp.mean(centred * centred, axis=-1, keepdims=True) + epsilon)
    return centred * inverse, inverse


def norm_back(upstream, normed, inverse, gain):
    scaled = upstream * gain
    centred = scaled - jnp.mean(scaled, axis=-1, keepdims=True)
    centred = centred - normed * jnp.mean(scaled * normed, axis=-1, keepdims=True)
    return centred * inverse


def column_sum(values):
    return jnp.sum(values, axis=0, keepdims=True)


def norm1_body(side, patches, halo, gain, bias, normed):
    rows = patches.shape[0]
    side_index = side[0]
    own_start = pl.multiple_of(side_index * HALO, HALO)
    halo_start = pl.multiple_of((1 - side_index) * rows, HALO)
    step = 128
    for first in range(0, rows, step):
        part = patches[first : first + step, :].astype(f32)
        xhat, _ = row_stats(part)
        normed[pl.ds(own_start + first, step), :] = (xhat * gain[...] + bias[...]).astype(bf16)
    for first in range(0, HALO, step):
        part = halo[first : first + step, :].astype(f32)
        xhat, _ = row_stats(part)
        normed[pl.ds(halo_start + first, step), :] = (xhat * gain[...] + bias[...]).astype(bf16)


def qkv_body(side, normed, weight, bias, queries, keys, values):
    rows = queries.shape[1]
    pairs = queries.shape[0]
    own_start = pl.multiple_of(side[0] * HALO, HALO)
    factor = 1.0 / math.sqrt(HEAD)
    ext = normed[...]
    own = normed[pl.ds(own_start, rows), :]
    part = (dot(own, weight[0]) + bias[0:1, :]).astype(bf16).astype(f32) * factor
    for pair in range(pairs):
        queries[pair] = part[:, pair * PAIR : (pair + 1) * PAIR].astype(bf16)
    part = dot(ext, weight[1])
    for pair in range(pairs):
        keys[pair] = part[:, pair * PAIR : (pair + 1) * PAIR].astype(bf16)
    part = dot(ext, weight[2]) + bias[1:2, :]
    for pair in range(pairs):
        values[pair] = part[:, pair * PAIR : (pair + 1) * PAIR].astype(bf16)


def first_qkv_kernel(side, patches, halo, gain, bias, weight, qbias, normed, queries, keys, values):
    norm1_body(side, patches, halo, gain, bias, normed)
    qkv_body(side, normed, weight, qbias, queries, keys, values)


def qkv_shapes(rows, width):
    pairs = width // PAIR
    ext = rows + HALO
    return (
        shape((pairs, rows, PAIR), bf16),
        shape((pairs, ext, PAIR), bf16),
        shape((pairs, ext, PAIR), bf16),
    )


def unit_table(side_index):
    return (
        ((2 - 2 * side_index) * BLOCK, 0, 5 * BLOCK),
        ((3 - 2 * side_index) * BLOCK, BLOCK, 5 * BLOCK),
        ((1 + side_index) * BLOCK, 2 * side_index * BLOCK, 4 * BLOCK),
        (3 * side_index * BLOCK, 3 * side_index * BLOCK, 3 * BLOCK),
    )


def aligned(value):
    if isinstance(value, int):
        return value
    return pl.multiple_of(value, BLOCK)


def pair_stack(block):
    lane = lax.broadcasted_iota(jnp.int32, block.shape, 1)
    zero = jnp.zeros_like(block)
    return jnp.concatenate(
        [jnp.where(lane < HEAD, block, zero), jnp.where(lane >= HEAD, block, zero)], axis=0
    )


def pair_merge(stacked):
    half = stacked.shape[0] // 2
    lane = lax.broadcasted_iota(jnp.int32, (half, stacked.shape[1]), 1)
    return jnp.where(lane < HEAD, stacked[:half], stacked[half:])


def mask_bias(side_index, pieces, images, first_query, first_key, key_count):
    base = side_index * HALO
    place = lax.broadcasted_iota(jnp.int32, (BLOCK, 1), 0) + (first_query + 2 * base)
    start = jnp.zeros_like(place)
    end = jnp.full_like(place, 2**30)
    running = jnp.int32(0)
    for image in range(images):
        running = running + pieces[image]
        start = jnp.where(place >= running, running, start)
        end = jnp.where(place < running, jnp.minimum(end, running), end)
    padding = place >= running
    start = jnp.where(padding, place, start)
    end = jnp.where(padding, place + 1, end)
    key_place = lax.broadcasted_iota(jnp.int32, (BLOCK, key_count), 1) + (first_key + base)
    return jnp.where((key_place >= start) & (key_place < end), 0.0, masked_score).astype(f32)


def attend_kernel(side, pieces, queries, keys, values, p0, p1, p2, p3, attended):
    side_index = side[0]
    pairs = queries.shape[0]
    images = pieces.shape[0] - 1
    for (first_query, first_key, count), shares_ref in zip(
        unit_table(side_index), (p0, p1, p2, p3)
    ):
        bias = mask_bias(side_index, pieces, images, first_query, first_key, count)
        query_rows = pl.ds(aligned(first_query), BLOCK)
        key_rows = pl.ds(aligned(first_key), count)
        for pair in range(pairs):
            stacked = pair_stack(queries[pair, query_rows, :])
            scores = dot_bt(stacked, keys[pair, key_rows, :])
            scores = (scores.reshape(2, BLOCK, count) + bias[None]).reshape(2 * BLOCK, count)
            weights = jnp.exp(scores - jnp.max(scores, axis=-1, keepdims=True))
            total = jnp.sum(weights, axis=-1, keepdims=True)
            shares = (weights * (1.0 / total)).astype(bf16)
            shares_ref[pair] = shares
            merged = pair_merge(dot(shares, values[pair, key_rows, :]))
            attended[query_rows, pair * PAIR : (pair + 1) * PAIR] = merged.astype(bf16)


def attend_back_kernel(
    side, queries, keys, values, p0, p1, p2, p3, upstream, grad_q, grad_k, grad_v, acc_k, acc_v
):
    side_index = side[0]
    pairs = queries.shape[0]
    factor = 1.0 / math.sqrt(HEAD)
    acc_k[...] = jnp.zeros_like(acc_k)
    acc_v[...] = jnp.zeros_like(acc_v)
    for (first_query, first_key, count), shares_ref in zip(
        unit_table(side_index), (p0, p1, p2, p3)
    ):
        query_rows = pl.ds(aligned(first_query), BLOCK)
        key_rows = pl.ds(aligned(first_key), count)
        for pair in range(pairs):
            columns = slice(pair * PAIR, (pair + 1) * PAIR)
            stacked_q = pair_stack(queries[pair, query_rows, :])
            stacked_g = pair_stack(upstream[query_rows, columns])
            shares = shares_ref[pair]
            wide_shares = shares.astype(f32)
            grad_shares = dot_bt(stacked_g, values[pair, key_rows, :])
            inner = jnp.sum(wide_shares * grad_shares, axis=-1, keepdims=True)
            grad_scores = (wide_shares * (grad_shares - inner)).astype(bf16)
            merged = pair_merge(dot(grad_scores, keys[pair, key_rows, :])) * factor
            grad_q[query_rows, columns] = merged.astype(bf16)
            acc_k[pair, key_rows, :] += dot_at(grad_scores, stacked_q)
            acc_v[pair, key_rows, :] += dot_at(shares, stacked_g)
    for pair in range(pairs):
        columns = slice(pair * PAIR, (pair + 1) * PAIR)
        grad_k[:, columns] = acc_k[pair].astype(bf16)
        grad_v[:, columns] = acc_v[pair].astype(bf16)


def project_kernel(
    att_own, att_par, w_own, w_par, out_bias, scale, patches, gain, bias, cotangent, mlp_scale,
    attn_proj, middle, normed2, grad_mlp,
):
    proj = dot(att_own[...], w_own[...]) + dot(att_par[...], w_par[...]) + out_bias[...]
    attn_proj[...] = proj
    mid = patches[...].astype(f32) + scale[...] * proj
    middle[...] = mid
    xhat, _ = row_stats(mid)
    normed2[...] = (xhat * gain[...] + bias[...]).astype(bf16)
    grad_mlp[...] = (cotangent[...].astype(f32) * mlp_scale[...]).astype(bf16)


def mlp_kernel(
    normed2, grad_mlp, w1_own, w1_par, b1_own, b1_par, w2_own, w2_par,
    dw1_own, dw1_par, dw2_own, dw2_par, db1_own, db1_par, dn2, mlp_out,
):
    step = pl.program_id(0)

    @pl.when(step == 0)
    def _():
        dn2[...] = jnp.zeros_like(dn2)
        mlp_out[...] = jnp.zeros_like(mlp_out)

    n2 = normed2[...]
    gm = grad_mlp[...]
    for w1, b1, w2, dw1, dw2, db1 in (
        (w1_par, b1_par, w2_par, dw1_par, dw2_par, db1_par),
        (w1_own, b1_own, w2_own, dw1_own, dw2_own, db1_own),
    ):
        before = dot(n2, w1[...]) + b1[...]
        grad_hidden = dot_bt(gm, w2[...])
        below = 0.5 + 0.5 * lax.erf(before * math.sqrt(0.5))
        density = jnp.exp(before * before * -0.5) * (1.0 / math.sqrt(2.0 * math.pi))
        hidden = (before * below).astype(bf16)
        grad_before = (grad_hidden * (below + before * density)).astype(bf16)
        dw2[...] = dot_at(hidden, gm).astype(bf16)
        dw1[...] = dot_at(n2, grad_before).astype(bf16)
        db1[...] = column_sum(grad_before.astype(f32))
        dn2[...] += dot_bt(grad_before, w1[...])
        mlp_out[...] += dot(hidden, w2[...])


def project_back_kernel(
    dn2_a, dn2_b, middle, cotangent, attn_proj, gain, scale, att_own, att_par, w_own, w_par,
    grad_middle, ga_own, ga_par, dwo_own, dwo_par, d_gain, d_bias, d_scale, d_out_bias,
):
    upstream = dn2_a[...] + dn2_b[...]
    xhat, inverse = row_stats(middle[...])
    d_gain[...] = column_sum(upstream * xhat)
    d_bias[...] = column_sum(upstream)
    grad_mid = cotangent[...].astype(f32) + norm_back(upstream, xhat, inverse, gain[...])
    grad_middle[...] = grad_mid
    d_scale[...] = column_sum(grad_mid * attn_proj[...])
    grad_proj = (grad_mid * scale[...]).astype(bf16)
    d_out_bias[...] = column_sum(grad_proj.astype(f32))
    width = att_own.shape[1]
    for att, weight, ga, dwo in (
        (att_own, w_own, ga_own, dwo_own),
        (att_par, w_par, ga_par, dwo_par),
    ):
        ga[...] = dot_bt(grad_proj, weight[...]).astype(bf16)
        full = dot_at(att[...], grad_proj).astype(bf16)
        for part in range(full.shape[1] // width):
            dwo[part * width : (part + 1) * width, :] = full[:, part * width : (part + 1) * width]


def qkv_back_kernel(
    side, normed, dq_own, dk_own, dv_own, dq_par, dk_par, dv_par, w_own, w_par, dwo_own, dwo_par,
    first_own, second_own, first_par, second_par, bias_own, bias_par, grad_own, grad_halo,
    total,
):
    rows = dq_own.shape[0]
    features = normed.shape[1]
    side_index = side[0]
    own_start = pl.multiple_of(side_index * HALO, HALO)
    halo_start = pl.multiple_of((1 - side_index) * rows, HALO)
    ext = normed[...]
    own = normed[pl.ds(own_start, rows), :]
    for dq, dk, dv, dwo, first, second, bias in (
        (dq_par, dk_par, dv_par, dwo_par, first_par, second_par, bias_par),
        (dq_own, dk_own, dv_own, dwo_own, first_own, second_own, bias_own),
    ):
        first[0:features, :] = dot_at(own, dq[...]).astype(bf16)
        first[features : 2 * features, :] = dot_at(ext, dk[...]).astype(bf16)
        second[0:features, :] = dot_at(ext, dv[...]).astype(bf16)
        second[features : 2 * features, :] = dwo[...]
        bias[0:1, :] = column_sum(dq[...].astype(f32))
        bias[1:2, :] = column_sum(dv[...].astype(f32))
    total[...] = (
        dot_bt(dk_own[...], w_own[1])
        + dot_bt(dv_own[...], w_own[2])
        + dot_bt(dk_par[...], w_par[1])
        + dot_bt(dv_par[...], w_par[2])
    )
    grad_halo[...] = total[pl.ds(halo_start, HALO), :].astype(bf16)
    grad_own[...] = (
        total[pl.ds(own_start, rows), :]
        + dot_bt(dq_own[...], w_own[0])
        + dot_bt(dq_par[...], w_par[0])
    )


def norm1_back_kernel(side, grad_own, grad_halo, patches, gain, grad_middle, out, d_gain, d_bias, total):
    start = pl.multiple_of((1 - side[0]) * (grad_own.shape[0] - HALO), HALO)
    total[...] = grad_own[...]
    total[pl.ds(start, HALO), :] += grad_halo[...].astype(f32)
    upstream = total[...]
    xhat, inverse = row_stats(patches[...].astype(f32))
    d_gain[...] = column_sum(upstream * xhat)
    d_bias[...] = column_sum(upstream)
    out[...] = grad_middle[...] + norm_back(upstream, xhat, inverse, gain[...])


def finish_kernel(mlp_a, mlp_b, middle, cotangent, grad_mlp, fc2_bias, scale, out, d_scale, d_bias):
    mlp_out = mlp_a[...] + mlp_b[...] + fc2_bias[...]
    out[...] = (middle[...] + scale[...] * mlp_out).astype(bf16)
    d_scale[...] = column_sum(cotangent[...].astype(f32) * mlp_out)
    d_bias[...] = column_sum(grad_mlp[...].astype(f32))


def wide_factors(size):
    lengths = []
    rest = size
    while rest % 4 == 0 and rest > 4:
        lengths.append(4)
        rest //= 4
    if rest == 4:
        lengths += [2, 2]
    elif rest > 1:
        lengths.append(rest)
    factors = []
    stride = size
    for length in lengths:
        stride //= length
        factors.append((length, stride))
    return factors


def shifted(size, factor, shift):
    length, stride = factor
    pairs = []
    for index in range(size):
        place = (index // stride) % length
        pairs.append((index, index + ((place + shift) % length - place) * stride))
    return pairs


def place_in(factor):
    length, stride = factor
    return (lax.axis_index("wide") // stride) % length


def send(value, factor, shift):
    return lax.ppermute(value, "wide", shifted(lax.axis_size("wide"), factor, shift))


def block_of(value, length, place):
    rows = value.shape[0] // length
    return lax.dynamic_slice_in_dim(value, place * rows, rows, 0)


def summed(terms):
    total = terms[0].astype(f32)
    for term in terms[1:]:
        total = total + term.astype(f32)
    return total


def scatter_terms(terms, factor):
    length, _ = factor
    place = place_in(factor)
    received = []
    for shift in range(1, length):
        target = (place + shift) % length
        part = summed([block_of(term, length, target) for term in terms]).astype(bf16)
        received.append(send(part, factor, shift))
    return [block_of(term, length, place) for term in terms] + received


def gather_block(value, factor):
    length, _ = factor
    place = place_in(factor)
    if length == 2:
        other = send(value, factor, 1)
        return jnp.where(
            place == 0,
            jnp.concatenate([value, other], axis=0),
            jnp.concatenate([other, value], axis=0),
        )
    rows = value.shape[0]
    whole = jnp.zeros((length * rows,) + value.shape[1:], value.dtype)
    whole = lax.dynamic_update_slice_in_dim(whole, value, place * rows, 0)
    for shift in range(1, length):
        other = send(value, factor, shift)
        source = (place - shift) % length
        whole = lax.dynamic_update_slice_in_dim(whole, other, source * rows, 0)
    return whole


def sum_over_wide(first_terms, second_terms):
    factors = wide_factors(lax.axis_size("wide"))[::-1]
    lead, rest = factors[:2], factors[2:]
    for factor in lead:
        first_terms = scatter_terms(first_terms, factor)
    for factor in lead[::-1]:
        second_terms = scatter_terms(second_terms, factor)
    columns = first_terms[0].shape[1]
    first, second = summed(first_terms).astype(bf16), summed(second_terms).astype(bf16)
    if rest:
        rows = first.shape[0]
        parts = 1
        for length, _ in rest:
            parts *= length
        merged = jnp.concatenate(
            [first.reshape(parts, rows // parts, columns), second.reshape(parts, rows // parts, columns)],
            axis=1,
        ).reshape(2 * rows, columns)
        terms = [merged]
        for factor in rest:
            terms = scatter_terms(terms, factor)
        merged = summed(terms).astype(bf16)
        for factor in rest[::-1]:
            merged = gather_block(merged, factor)
        merged = merged.reshape(parts, 2, rows // parts, columns)
        first = merged[:, 0].reshape(rows, columns)
        second = merged[:, 1].reshape(rows, columns)
    for factor in lead[::-1]:
        first = gather_block(first, factor)
    for factor in lead:
        second = gather_block(second, factor)
    return first, second


def sum_small(vector):
    for factor in wide_factors(lax.axis_size("wide"))[::-1]:
        vector = summed([vector] + [send(vector, factor, s) for s in range(1, factor[0])])
    return vector


def on_device(
    patches,
    pieces,
    ln1_gain,
    ln1_bias,
    qkv_weight,
    qkv_bias,
    out_weight,
    out_bias,
    attn_scale,
    ln2_gain,
    ln2_bias,
    fc1_weight,
    fc1_bias,
    fc2_weight,
    fc2_bias,
    mlp_scale,
    cotangent,
):
    rows, features = patches.shape
    width = out_weight.shape[0]
    hidden_half = fc1_weight.shape[1]
    pairs = width // PAIR
    ext = rows + HALO
    side_index = lax.axis_index("narrow")
    side = side_index.astype(jnp.int32).reshape(1)
    pieces_row = pieces.reshape(-1)
    swap = [(0, 1), (1, 0)]

    def other(value):
        return lax.ppermute(value, "narrow", swap)

    def row(vector):
        return vector.reshape(1, -1)

    halo = other(lax.dynamic_slice_in_dim(patches, (1 - side_index) * (rows - HALO), HALO, 0))
    qkv_par = other(qkv_weight)
    small_par = other(jnp.concatenate([qkv_bias.reshape(-1), fc1_bias]))
    out_par = other(out_weight)
    fc1_par = other(fc1_weight)
    fc2_par = other(fc2_weight)
    qkv_bias_par = small_par[: 2 * width].reshape(2, width)
    fc1_bias_par = small_par[2 * width :]

    gain1, bias1 = row(ln1_gain), row(ln1_bias)
    gain2, bias2 = row(ln2_gain), row(ln2_bias)

    qkv_flops = 2 * features * width * (rows + 2 * ext)
    normed1, q_own, k_own, v_own = pl.pallas_call(
        first_qkv_kernel,
        out_shape=(shape((ext, features), bf16),) + qkv_shapes(rows, width),
        in_specs=[SCALARS] + [WHOLE] * 6,
        out_specs=(WHOLE,) * 4,
        compiler_params=params(),
        cost_estimate=cost(qkv_flops, 8e6),
        name="qkv_own",
    )(side, patches, halo, gain1, bias1, qkv_weight, qkv_bias)

    def shares_shapes():
        return tuple(
            shape((pairs, 2 * BLOCK, count), bf16) for _, _, count in unit_table(0)
        )

    area = sum(count for _, _, count in unit_table(0)) * BLOCK * 2 * pairs

    def attend(q, k, v, name):
        return pl.pallas_call(
            attend_kernel,
            out_shape=shares_shapes() + (shape((rows, width), bf16),),
            in_specs=[SCALARS, SCALARS] + [WHOLE] * 3,
            out_specs=(WHOLE,) * 5,
            compiler_params=params(),
            cost_estimate=cost(4 * area * PAIR, 6e6, area),
            name=name,
        )(side, pieces_row, q, k, v)

    *shares_own, att_own = attend(q_own, k_own, v_own, "attend_own")
    q_par, k_par, v_par = pl.pallas_call(
        qkv_body,
        out_shape=qkv_shapes(rows, width),
        in_specs=[SCALARS] + [WHOLE] * 3,
        out_specs=(WHOLE,) * 3,
        compiler_params=params(),
        cost_estimate=cost(qkv_flops, 6e6),
        name="qkv_par",
    )(side, normed1, qkv_par, qkv_bias_par)
    *shares_par, att_par = attend(q_par, k_par, v_par, "attend_par")

    steps = 2
    block = rows // steps
    by_row = pl.BlockSpec((block, features), lambda i: (i, 0))
    att_row = pl.BlockSpec((block, width), lambda i: (i, 0))
    w_spec = pl.BlockSpec((width, features), lambda i: (0, 0))
    vec = pl.BlockSpec((1, features), lambda i: (0, 0))
    attn_proj, middle, normed2, grad_mlp = pl.pallas_call(
        project_kernel,
        grid=(steps,),
        out_shape=(
            shape((rows, features), f32),
            shape((rows, features), f32),
            shape((rows, features), bf16),
            shape((rows, features), bf16),
        ),
        in_specs=[att_row, att_row, w_spec, w_spec, vec, vec, by_row, vec, vec, by_row, vec],
        out_specs=(by_row,) * 4,
        compiler_params=params(),
        cost_estimate=cost(4 * rows * width * features, 9e6),
        name="project",
    )(
        att_own, att_par, out_weight, out_par, row(out_bias), row(attn_scale), patches, gain2, bias2,
        cotangent, row(mlp_scale),
    )

    chunks = 2
    per_chunk = hidden_half // chunks
    fb = per_chunk // 2

    def mlp(chunk):
        first = chunk * 2
        const = pl.BlockSpec((rows, features), lambda j: (0, 0))
        w1_spec = pl.BlockSpec((features, fb), lambda j: (0, first + j))
        b1_spec = pl.BlockSpec((1, fb), lambda j: (0, first + j))
        w2_spec = pl.BlockSpec((fb, features), lambda j: (first + j, 0))
        d1_spec = pl.BlockSpec((features, fb), lambda j: (0, j))
        d2_spec = pl.BlockSpec((fb, features), lambda j: (j, 0))
        db_spec = pl.BlockSpec((1, fb), lambda j: (0, j))
        return pl.pallas_call(
            mlp_kernel,
            grid=(2,),
            out_shape=(
                shape((features, per_chunk), bf16),
                shape((features, per_chunk), bf16),
                shape((per_chunk, features), bf16),
                shape((per_chunk, features), bf16),
                shape((1, per_chunk), f32),
                shape((1, per_chunk), f32),
                shape((rows, features), f32),
                shape((rows, features), f32),
            ),
            in_specs=[const, const, w1_spec, w1_spec, b1_spec, b1_spec, w2_spec, w2_spec],
            out_specs=(d1_spec, d1_spec, d2_spec, d2_spec, db_spec, db_spec, const, const),
            compiler_params=params(),
            cost_estimate=cost(
                12 * rows * features * 2 * per_chunk, 16e6, 4 * rows * per_chunk
            ),
            name="mlp_%d" % chunk,
        )(
            normed2, grad_mlp, fc1_weight, fc1_par, row(fc1_bias), row(fc1_bias_par), fc2_weight,
            fc2_par,
        )

    mlp_results = [mlp(chunk) for chunk in range(chunks)]
    mlp_sums = []
    for dw1_own, dw1_par, dw2_own, dw2_par, *_ in mlp_results:
        mlp_sums.append(sum_over_wide([dw2_own, other(dw2_par)], [dw1_own, other(dw1_par)]))

    small = shape((1, features), f32)
    (
        grad_middle, ga_own, ga_par, dwo_own, dwo_par, d_gain2, d_bias2, d_attn_scale, d_out_bias,
    ) = pl.pallas_call(
        project_back_kernel,
        out_shape=(
            shape((rows, features), f32),
            shape((rows, width), bf16),
            shape((rows, width), bf16),
            shape((features, width), bf16),
            shape((features, width), bf16),
            small, small, small, small,
        ),
        in_specs=[WHOLE] * 11,
        out_specs=(WHOLE,) * 9,
        compiler_params=params(),
        cost_estimate=cost(8 * rows * width * features, 16e6),
        name="project_back",
    )(
        mlp_results[0][6], mlp_results[1][6], middle, cotangent, attn_proj, gain2, row(attn_scale),
        att_own, att_par, out_weight, out_par,
    )

    def attend_back(q, k, v, shares, ga, name):
        return pl.pallas_call(
            attend_back_kernel,
            out_shape=(
                shape((rows, width), bf16),
                shape((ext, width), bf16),
                shape((ext, width), bf16),
            ),
            in_specs=[SCALARS] + [WHOLE] * 8,
            out_specs=(WHOLE,) * 3,
            scratch_shapes=[
                pltpu.VMEM((pairs, ext, PAIR), f32),
                pltpu.VMEM((pairs, ext, PAIR), f32),
            ],
            compiler_params=params(),
            cost_estimate=cost(8 * area * PAIR, 8e6),
            name=name,
        )(side, q, k, v, *shares, ga)

    dq_own, dk_own, dv_own = attend_back(q_own, k_own, v_own, shares_own, ga_own, "attend_back_own")
    dq_par, dk_par, dv_par = attend_back(q_par, k_par, v_par, shares_par, ga_par, "attend_back_par")

    pack = shape((2 * features, width), bf16)
    (
        first_own, second_own, first_par, second_par, qb_own, qb_par, grad_own, grad_halo,
    ) = pl.pallas_call(
        qkv_back_kernel,
        out_shape=(
            pack, pack, pack, pack,
            shape((2, width), f32), shape((2, width), f32),
            shape((rows, features), f32), shape((HALO, features), bf16),
        ),
        in_specs=[SCALARS] + [WHOLE] * 11,
        out_specs=(WHOLE,) * 8,
        scratch_shapes=[pltpu.VMEM((ext, features), f32)],
        compiler_params=params(),
        cost_estimate=cost(4 * qkv_flops, 24e6),
        name="qkv_back",
    )(
        side, normed1, dq_own, dk_own, dv_own, dq_par, dk_par, dv_par, qkv_weight, qkv_par, dwo_own,
        dwo_par,
    )
    halo_back = other(grad_halo)
    qkv_sums = sum_over_wide([first_own, other(first_par)], [second_own, other(second_par)])

    grad_patches, d_gain1, d_bias1 = pl.pallas_call(
        norm1_back_kernel,
        out_shape=(shape((rows, features), f32), small, small),
        in_specs=[SCALARS] + [WHOLE] * 5,
        out_specs=(WHOLE,) * 3,
        scratch_shapes=[pltpu.VMEM((rows, features), f32)],
        compiler_params=params(),
        cost_estimate=cost(20 * rows * features, 6e6),
        name="norm1_back",
    )(side, grad_own, halo_back, patches, gain1, grad_middle)

    output, d_mlp_scale, d_fc2_bias = pl.pallas_call(
        finish_kernel,
        out_shape=(shape((rows, features), bf16), small, small),
        in_specs=[WHOLE] * 7,
        out_specs=(WHOLE,) * 3,
        compiler_params=params(),
        cost_estimate=cost(20 * rows * features, 8e6),
        name="finish",
    )(
        mlp_results[0][7], mlp_results[1][7], middle, cotangent, grad_mlp, row(fc2_bias),
        row(mlp_scale),
    )

    shared = [d_gain1, d_bias1, d_attn_scale, d_out_bias, d_gain2, d_bias2, d_mlp_scale, d_fc2_bias]
    half_own = [qb_own.reshape(1, -1), mlp_results[0][4], mlp_results[1][4]]
    half_par = [qb_par.reshape(1, -1), mlp_results[0][5], mlp_results[1][5]]
    mine = jnp.concatenate(shared + half_own, axis=1).reshape(-1)
    theirs = jnp.concatenate(shared + half_par, axis=1).reshape(-1)
    vectors = sum_small(mine + other(theirs))
    shared_sums = vectors[: 8 * features].reshape(8, features)
    half_sums = vectors[8 * features :]
    grad_qkv_bias = half_sums[: 2 * width].reshape(2, width)
    grad_fc1_bias = half_sums[2 * width :]

    grad_fc2_weight = jnp.concatenate([s[0] for s in mlp_sums], axis=0).astype(f32)
    grad_fc1_weight = jnp.concatenate([s[1] for s in mlp_sums], axis=1).astype(f32)
    first, second = qkv_sums
    grad_qkv_weight = (
        jnp.concatenate([first, second[:features]], axis=0).astype(f32).reshape(3, features, width)
    )
    tail = second[features:].astype(f32)
    grad_out_weight = jnp.concatenate(
        [tail[part * width : (part + 1) * width] for part in range(features // width)], axis=1
    )
    return (
        output,
        grad_patches,
        shared_sums[0],
        shared_sums[1],
        grad_qkv_weight,
        grad_qkv_bias,
        grad_out_weight,
        shared_sums[3],
        shared_sums[2],
        shared_sums[4],
        shared_sums[5],
        grad_fc1_weight,
        grad_fc1_bias,
        grad_fc2_weight,
        shared_sums[7],
        shared_sums[6],
    )


def solution(mesh):
    in_specs = (
        P(("wide", "narrow"), None),
        P("wide", None),
        P(),
        P(),
        P(None, None, "narrow"),
        P(None, "narrow"),
        P("narrow", None),
        P(),
        P(),
        P(),
        P(),
        P(None, "narrow"),
        P("narrow"),
        P("narrow", None),
        P(),
        P(),
        P(("wide", "narrow"), None),
    )
    out_specs = (
        P(("wide", "narrow"), None),
        P(("wide", "narrow"), None),
        P(),
        P(),
        P(None, None, "narrow"),
        P(None, "narrow"),
        P("narrow", None),
        P(),
        P(),
        P(),
        P(),
        P(None, "narrow"),
        P("narrow"),
        P("narrow", None),
        P(),
        P(),
    )
    return jax.shard_map(
        on_device, mesh=mesh, in_specs=in_specs, out_specs=out_specs, check_vma=False
    )
```

```python
from functools import partial
import math

import jax
import jax.numpy as jnp
from jax import lax
from jax.sharding import PartitionSpec as P
from jax.experimental import pallas as pl
from jax.experimental.pallas import tpu as pltpu

HEAD = 64
PAIR = 2 * HEAD
HALO = 256
BLOCK = 128

epsilon = 1e-06
masked_score = -1e30

bf16 = jnp.bfloat16
f32 = jnp.float32

WHOLE = pl.BlockSpec(memory_space=pltpu.VMEM)
SCALARS = pl.BlockSpec(memory_space=pltpu.SMEM)


def params(mib=56):
    return pltpu.CompilerParams(vmem_limit_bytes=mib * 1024 * 1024)


def cost(flops, nbytes, transcendentals=0):
    return pl.CostEstimate(
        flops=int(flops), bytes_accessed=int(nbytes), transcendentals=int(transcendentals)
    )


def shape(dims, dtype):
    return jax.ShapeDtypeStruct(dims, dtype)


def dot(a, b):
    return jnp.dot(a, b, preferred_element_type=f32)


def dot_bt(a, b):
    return lax.dot_general(a, b, (((1,), (1,)), ((), ())), preferred_element_type=f32)


def dot_at(a, b):
    return lax.dot_general(a, b, (((0,), (0,)), ((), ())), preferred_element_type=f32)


def row_stats(values):
    average = jnp.mean(values, axis=-1, keepdims=True)
    centred = values - average
    inverse = lax.rsqrt(jnp.mean(centred * centred, axis=-1, keepdims=True) + epsilon)
    return centred * inverse, inverse


def norm_back(upstream, normed, inverse, gain):
    scaled = upstream * gain
    centred = scaled - jnp.mean(scaled, axis=-1, keepdims=True)
    centred = centred - normed * jnp.mean(scaled * normed, axis=-1, keepdims=True)
    return centred * inverse


def flat(vector):
    return vector[...].reshape(1, -1)


def column_sum(values):
    return jnp.sum(values, axis=0, keepdims=True)


def norm1_body(side, patches, halo, gain, bias, normed):
    rows = patches.shape[0]
    side_index = side[0]
    own_start = pl.multiple_of(side_index * HALO, HALO)
    halo_start = pl.multiple_of((1 - side_index) * rows, HALO)
    step = 128
    for first in range(0, rows, step):
        part = patches[first : first + step, :].astype(f32)
        xhat, _ = row_stats(part)
        normed[pl.ds(own_start + first, step), :] = (xhat * flat(gain) + flat(bias)).astype(bf16)
    for first in range(0, HALO, step):
        part = halo[first : first + step, :].astype(f32)
        xhat, _ = row_stats(part)
        normed[pl.ds(halo_start + first, step), :] = (xhat * flat(gain) + flat(bias)).astype(bf16)


def qkv_body(side, normed, weight, bias, queries, keys, values):
    rows = queries.shape[1]
    pairs = queries.shape[0]
    own_start = pl.multiple_of(side[0] * HALO, HALO)
    factor = 1.0 / math.sqrt(HEAD)
    ext = normed[...]
    own = normed[pl.ds(own_start, rows), :]
    part = (dot(own, weight[0]) + bias[0:1, :]).astype(bf16).astype(f32) * factor
    for pair in range(pairs):
        queries[pair] = part[:, pair * PAIR : (pair + 1) * PAIR].astype(bf16)
    part = dot(ext, weight[1])
    for pair in range(pairs):
        keys[pair] = part[:, pair * PAIR : (pair + 1) * PAIR].astype(bf16)
    part = dot(ext, weight[2]) + bias[1:2, :]
    for pair in range(pairs):
        values[pair] = part[:, pair * PAIR : (pair + 1) * PAIR].astype(bf16)


def first_qkv_kernel(side, patches, halo, gain, bias, weight, qbias, normed, queries, keys, values):
    norm1_body(side, patches, halo, gain, bias, normed)
    qkv_body(side, normed, weight, qbias, queries, keys, values)


def qkv_shapes(rows, width):
    pairs = width // PAIR
    ext = rows + HALO
    return (
        shape((pairs, rows, PAIR), bf16),
        shape((pairs, ext, PAIR), bf16),
        shape((pairs, ext, PAIR), bf16),
    )


def unit_table(side_index):
    return (
        ((2 - 2 * side_index) * BLOCK, 0, 5 * BLOCK),
        ((3 - 2 * side_index) * BLOCK, BLOCK, 5 * BLOCK),
        ((1 + side_index) * BLOCK, 2 * side_index * BLOCK, 4 * BLOCK),
        (3 * side_index * BLOCK, 3 * side_index * BLOCK, 3 * BLOCK),
    )


def aligned(value):
    if isinstance(value, int):
        return value
    return pl.multiple_of(value, BLOCK)


def pair_stack(block):
    lane = lax.broadcasted_iota(jnp.int32, block.shape, 1)
    zero = jnp.zeros_like(block)
    return jnp.concatenate(
        [jnp.where(lane < HEAD, block, zero), jnp.where(lane >= HEAD, block, zero)], axis=0
    )


def pair_merge(stacked):
    half = stacked.shape[0] // 2
    lane = lax.broadcasted_iota(jnp.int32, (half, stacked.shape[1]), 1)
    return jnp.where(lane < HEAD, stacked[:half], stacked[half:])


def mask_bias(side_index, pieces, images, first_query, first_key, key_count):
    base = side_index * HALO
    place = lax.broadcasted_iota(jnp.int32, (BLOCK, 1), 0) + (first_query + 2 * base)
    start = jnp.zeros_like(place)
    end = jnp.full_like(place, 2**30)
    running = jnp.int32(0)
    for image in range(images):
        running = running + pieces[image]
        start = jnp.where(place >= running, running, start)
        end = jnp.where(place < running, jnp.minimum(end, running), end)
    padding = place >= running
    start = jnp.where(padding, place, start)
    end = jnp.where(padding, place + 1, end)
    key_place = lax.broadcasted_iota(jnp.int32, (BLOCK, key_count), 1) + (first_key + base)
    return jnp.where((key_place >= start) & (key_place < end), 0.0, masked_score).astype(f32)


def attend_kernel(side, pieces, queries, keys, values, p0, p1, p2, p3, attended):
    side_index = side[0]
    pairs = queries.shape[0]
    images = pieces.shape[0] - 1
    for (first_query, first_key, count), shares_ref in zip(
        unit_table(side_index), (p0, p1, p2, p3)
    ):
        bias = mask_bias(side_index, pieces, images, first_query, first_key, count)
        query_rows = pl.ds(aligned(first_query), BLOCK)
        key_rows = pl.ds(aligned(first_key), count)
        for pair in range(pairs):
            stacked = pair_stack(queries[pair, query_rows, :])
            scores = dot_bt(stacked, keys[pair, key_rows, :])
            scores = (scores.reshape(2, BLOCK, count) + bias[None]).reshape(2 * BLOCK, count)
            weights = jnp.exp(scores - jnp.max(scores, axis=-1, keepdims=True))
            total = jnp.sum(weights, axis=-1, keepdims=True)
            shares = (weights * (1.0 / total)).astype(bf16)
            shares_ref[pair] = shares
            merged = pair_merge(dot(shares, values[pair, key_rows, :]))
            attended[query_rows, pair * PAIR : (pair + 1) * PAIR] = merged.astype(bf16)


def attend_back_kernel(
    side, queries, keys, values, p0, p1, p2, p3, upstream, grad_q, grad_k, grad_v, acc_k, acc_v
):
    side_index = side[0]
    pairs = queries.shape[0]
    factor = 1.0 / math.sqrt(HEAD)
    acc_k[...] = jnp.zeros_like(acc_k)
    acc_v[...] = jnp.zeros_like(acc_v)
    for (first_query, first_key, count), shares_ref in zip(
        unit_table(side_index), (p0, p1, p2, p3)
    ):
        query_rows = pl.ds(aligned(first_query), BLOCK)
        key_rows = pl.ds(aligned(first_key), count)
        for pair in range(pairs):
            columns = slice(pair * PAIR, (pair + 1) * PAIR)
            stacked_q = pair_stack(queries[pair, query_rows, :])
            stacked_g = pair_stack(upstream[query_rows, columns])
            shares = shares_ref[pair]
            wide_shares = shares.astype(f32)
            grad_shares = dot_bt(stacked_g, values[pair, key_rows, :])
            inner = jnp.sum(wide_shares * grad_shares, axis=-1, keepdims=True)
            grad_scores = (wide_shares * (grad_shares - inner)).astype(bf16)
            merged = pair_merge(dot(grad_scores, keys[pair, key_rows, :])) * factor
            grad_q[query_rows, columns] = merged.astype(bf16)
            acc_k[pair, key_rows, :] += dot_at(grad_scores, stacked_q)
            acc_v[pair, key_rows, :] += dot_at(shares, stacked_g)
    for pair in range(pairs):
        columns = slice(pair * PAIR, (pair + 1) * PAIR)
        grad_k[:, columns] = acc_k[pair].astype(bf16)
        grad_v[:, columns] = acc_v[pair].astype(bf16)


def project_kernel(
    att_own, att_par, w_own, w_par, out_bias, scale, patches, gain, bias, cotangent, mlp_scale,
    attn_proj, middle, normed2, grad_mlp,
):
    proj = dot(att_own[...], w_own[...]) + dot(att_par[...], w_par[...]) + flat(out_bias)
    attn_proj[...] = proj
    mid = patches[...].astype(f32) + flat(scale) * proj
    middle[...] = mid
    xhat, _ = row_stats(mid)
    normed2[...] = (xhat * flat(gain) + flat(bias)).astype(bf16)
    grad_mlp[...] = (cotangent[...].astype(f32) * flat(mlp_scale)).astype(bf16)


def mlp_kernel(
    normed2, grad_mlp, w1_own, w1_par, b1_own, b1_par, w2_own, w2_par,
    pack_own, pack_par, db1_own, db1_par, dn2, mlp_out, *, first_bias,
):
    step = pl.program_id(0)

    @pl.when(step == 0)
    def _():
        dn2[...] = jnp.zeros_like(dn2)
        mlp_out[...] = jnp.zeros_like(mlp_out)

    n2 = normed2[...]
    gm = grad_mlp[...]
    fb = w2_own.shape[0]
    half = pack_own.shape[0] // 2
    place = pl.ds(pl.multiple_of(step * fb, 128), fb)
    bias_place = pl.ds(pl.multiple_of(step * fb + first_bias, 128), fb)
    for w1, b1, w2, pack, db1 in (
        (w1_par, b1_par, w2_par, pack_par, db1_par),
        (w1_own, b1_own, w2_own, pack_own, db1_own),
    ):
        before = dot(n2, w1[...]) + b1[:, bias_place]
        grad_hidden = dot_bt(gm, w2[...])
        below = 0.5 + 0.5 * lax.erf(before * math.sqrt(0.5))
        density = jnp.exp(before * before * -0.5) * (1.0 / math.sqrt(2.0 * math.pi))
        hidden = (before * below).astype(bf16)
        grad_before = (grad_hidden * (below + before * density)).astype(bf16)
        pack[place, :] = dot_at(hidden, gm).astype(bf16)
        pack[half:, place] = dot_at(n2, grad_before).astype(bf16)
        db1[:, place] = column_sum(grad_before.astype(f32))
        dn2[...] += dot_bt(grad_before, w1[...])
        mlp_out[...] += dot(hidden, w2[...])


def project_back_kernel(
    dn2_a, dn2_b, middle, cotangent, attn_proj, gain, scale, att_own, att_par, w_own, w_par,
    grad_middle, ga_own, ga_par, dwo_own, dwo_par, d_gain, d_bias, d_scale, d_out_bias,
):
    upstream = dn2_a[...] + dn2_b[...]
    xhat, inverse = row_stats(middle[...])
    d_gain[...] = column_sum(upstream * xhat)
    d_bias[...] = column_sum(upstream)
    grad_mid = cotangent[...].astype(f32) + norm_back(upstream, xhat, inverse, flat(gain))
    grad_middle[...] = grad_mid
    d_scale[...] = column_sum(grad_mid * attn_proj[...])
    grad_proj = (grad_mid * flat(scale)).astype(bf16)
    d_out_bias[...] = column_sum(grad_proj.astype(f32))
    width = att_own.shape[1]
    for att, weight, ga, dwo in (
        (att_own, w_own, ga_own, dwo_own),
        (att_par, w_par, ga_par, dwo_par),
    ):
        ga[...] = dot_bt(grad_proj, weight[...]).astype(bf16)
        full = dot_at(att[...], grad_proj).astype(bf16)
        for part in range(full.shape[1] // width):
            dwo[part * width : (part + 1) * width, :] = full[:, part * width : (part + 1) * width]


def qkv_back_kernel(
    side, normed, dq_own, dk_own, dv_own, dq_par, dk_par, dv_par, w_own, w_par, dwo_own, dwo_par,
    pack_own, pack_par, bias_own, bias_par, grad_own, grad_halo, total,
):
    rows = dq_own.shape[0]
    features = normed.shape[1]
    side_index = side[0]
    own_start = pl.multiple_of(side_index * HALO, HALO)
    halo_start = pl.multiple_of((1 - side_index) * rows, HALO)
    ext = normed[...]
    own = normed[pl.ds(own_start, rows), :]
    for dq, dk, dv, dwo, pack, bias in (
        (dq_par, dk_par, dv_par, dwo_par, pack_par, bias_par),
        (dq_own, dk_own, dv_own, dwo_own, pack_own, bias_own),
    ):
        pack[0:features, :] = dot_at(own, dq[...]).astype(bf16)
        pack[features : 2 * features, :] = dot_at(ext, dk[...]).astype(bf16)
        pack[2 * features : 3 * features, :] = dot_at(ext, dv[...]).astype(bf16)
        pack[3 * features : 4 * features, :] = dwo[...]
        bias[0:1, :] = column_sum(dq[...].astype(f32))
        bias[1:2, :] = column_sum(dv[...].astype(f32))
    total[...] = (
        dot_bt(dk_own[...], w_own[1])
        + dot_bt(dv_own[...], w_own[2])
        + dot_bt(dk_par[...], w_par[1])
        + dot_bt(dv_par[...], w_par[2])
    )
    grad_halo[...] = total[pl.ds(halo_start, HALO), :].astype(bf16)
    grad_own[...] = (
        total[pl.ds(own_start, rows), :]
        + dot_bt(dq_own[...], w_own[0])
        + dot_bt(dq_par[...], w_par[0])
    )


def norm1_back_kernel(side, grad_own, grad_halo, patches, gain, grad_middle, out, d_gain, d_bias, total):
    start = pl.multiple_of((1 - side[0]) * (grad_own.shape[0] - HALO), HALO)
    total[...] = grad_own[...]
    total[pl.ds(start, HALO), :] += grad_halo[...].astype(f32)
    upstream = total[...]
    xhat, inverse = row_stats(patches[...].astype(f32))
    d_gain[...] = column_sum(upstream * xhat)
    d_bias[...] = column_sum(upstream)
    out[...] = grad_middle[...] + norm_back(upstream, xhat, inverse, flat(gain))


VECTOR_ROWS = 16


def finish_kernel(
    mlp_a, mlp_b, middle, cotangent, grad_mlp, fc2_bias, scale, d_gain1, d_bias1, d_gain2, d_bias2,
    d_attn_scale, d_out_bias, qb_own, qb_par, b1a_own, b1a_par, b1b_own, b1b_par,
    out, mine, theirs,
):
    mlp_out = mlp_a[...] + mlp_b[...] + flat(fc2_bias)
    out[...] = (middle[...] + flat(scale) * mlp_out).astype(bf16)
    d_scale = column_sum(cotangent[...].astype(f32) * mlp_out)
    d_bias = column_sum(grad_mlp[...].astype(f32))
    features = middle.shape[1]
    width = qb_own.shape[1]
    for pack, qb, b1a, b1b in ((mine, qb_own, b1a_own, b1b_own), (theirs, qb_par, b1a_par, b1b_par)):
        pack[...] = jnp.zeros_like(pack)
        for index, vector in enumerate((d_gain1, d_bias1, d_gain2, d_bias2, d_attn_scale, d_out_bias)):
            pack[index : index + 1, :] = vector[...]
        pack[6:7, :] = d_scale
        pack[7:8, :] = d_bias
        pack[8:9, 0:width] = qb[0:1, :]
        pack[9:10, 0:width] = qb[1:2, :]
        pack[10:11, 0:features] = b1a[...]
        pack[11:12, 0:features] = b1b[...]


def unpack_kernel(
    *refs, terms, deps
):
    total = refs[0][...]
    for index in range(1, terms):
        total = total + refs[index][...]
    (
        d_gain1, d_bias1, d_gain2, d_bias2, d_attn_scale, d_out_bias, d_scale, d_bias, qb, b1,
    ) = refs[terms + deps :]
    for index, out in enumerate(
        (d_gain1, d_bias1, d_gain2, d_bias2, d_attn_scale, d_out_bias, d_scale, d_bias)
    ):
        out[...] = total[index]
    width = qb.shape[1]
    qb[0:1, :] = total[8:9, 0:width]
    qb[1:2, :] = total[9:10, 0:width]
    half = b1.shape[0] // 2
    b1[0:half] = total[10]
    b1[half:] = total[11]


def add_kernel(*refs, terms):
    total = refs[0][...]
    for index in range(1, terms):
        total = total + refs[index][...]
    refs[-1][...] = total


def wide_factors(size):
    lengths = []
    rest = size
    while rest % 4 == 0 and rest > 4:
        lengths.append(4)
        rest //= 4
    if rest == 4:
        lengths += [2, 2]
    elif rest > 1:
        lengths.append(rest)
    factors = []
    stride = size
    for length in lengths:
        stride //= length
        factors.append((length, stride))
    return factors[::-1]


def place_in(factor):
    length, stride = factor
    return (lax.axis_index("wide") // stride) % length


class Axis:
    def __init__(self, even, odd):
        self.even, self.odd = even, odd
        self.length = even[0]
        side = lax.axis_index("narrow")
        self.place = jnp.where(side == 0, place_in(even), place_in(odd)).astype(jnp.int32)

    def send(self, value, shift):
        pairs = []
        groups = lax.axis_size("narrow")
        for index in range(lax.axis_size("wide")):
            for side in range(groups):
                length, stride = self.odd if side else self.even
                here = (index // stride) % length
                target = index + ((here + shift) % length - here) * stride
                pairs.append((index * groups + side, target * groups + side))
        return lax.ppermute(value, ("wide", "narrow"), pairs)


def wide_axes():
    factors = wide_factors(lax.axis_size("wide"))
    if len(factors) > 1 and factors[0][0] == factors[1][0]:
        first, second = factors[:2]
        return [Axis(first, second), Axis(second, first)] + [Axis(f, f) for f in factors[2:]]
    return [Axis(f, f) for f in factors]


ANY = pl.BlockSpec(memory_space=pl.ANY)


def combine_kernel(starts, *refs, terms, outs, deps):
    for out in range(outs):
        total = refs[out * terms][...].astype(f32)
        for term in range(1, terms):
            total = total + refs[out * terms + term][...].astype(f32)
        refs[outs * terms + deps + out][...] = total.astype(bf16)


def combine(terms, rows, blocks, deps, name):
    columns = terms[0][0].shape[1]
    tile = rows
    while tile * columns > 256 * 768 and tile % 32 == 0:
        tile //= 2
    starts = jnp.stack(
        [((offset + block * rows) // tile).astype(jnp.int32) for block in blocks for _, offset in terms]
    )
    count = len(blocks) * len(terms)
    out_spec = pl.BlockSpec((tile, columns), lambda g, s: (g, 0))
    return pl.pallas_call(
        partial(combine_kernel, terms=len(terms), outs=len(blocks), deps=len(deps)),
        out_shape=[shape((rows, columns), bf16)] * len(blocks),
        grid_spec=pltpu.PrefetchScalarGridSpec(
            num_scalar_prefetch=1,
            grid=(rows // tile,),
            in_specs=[
                pl.BlockSpec((tile, columns), lambda g, s, i=i: (s[i] + g, 0)) for i in range(count)
            ]
            + [ANY] * len(deps),
            out_specs=[out_spec] * len(blocks),
        ),
        compiler_params=params(32),
        cost_estimate=cost(count * rows * columns, (count + 1) * rows * columns * 2),
        name=name,
    )(starts, *[term for _ in blocks for term, _ in terms], *deps)


def assemble_kernel(starts, *refs, count, deps):
    out = refs[count + deps]
    rows = refs[0].shape[0]
    for index in range(count):
        out[pl.ds(pl.multiple_of(starts[index], 16), rows), :] = refs[index][...]


def assemble(blocks, places, deps, name):
    rows, columns = blocks[0].shape
    starts = jnp.stack([(place * rows).astype(jnp.int32) for place in places])
    return pl.pallas_call(
        partial(assemble_kernel, count=len(blocks), deps=len(deps)),
        out_shape=shape((rows * len(blocks), columns), bf16),
        in_specs=[SCALARS] + [WHOLE] * len(blocks) + [ANY] * len(deps),
        out_specs=WHOLE,
        compiler_params=params(32),
        cost_estimate=cost(rows * columns, 4 * rows * len(blocks) * columns),
        name=name,
    )(starts, *blocks, *deps)


class GroupSum:
    def __init__(self, own, received, axes, name):
        self.terms = [(own, jnp.int32(0)), (received, jnp.int32(0))]
        self.rows = own.shape[0]
        self.axes = axes
        self.name = name
        self.stage = 0
        self.split = []
        self.halves = None

    def scatter(self, deps):
        axis = self.axes[self.stage]
        name = "%s_s%d" % (self.name, self.stage)
        self.stage += 1
        length = axis.length
        rows = self.rows // length
        if self.rows % length or rows % 16:
            (total,) = combine(self.terms, self.rows, [jnp.int32(0)], deps, name)
            zero = jnp.int32(0)
            self.terms = [(total, zero)]
            self.terms += [(axis.send(total, shift), zero) for shift in range(1, length)]
            return total
        blocks = [(axis.place + shift) % length for shift in range(1, length)]
        sends = combine(self.terms, rows, blocks, deps, name)
        self.terms = [(term, offset + axis.place * rows) for term, offset in self.terms]
        for shift, block in enumerate(sends, 1):
            self.terms.append((axis.send(block, shift), jnp.int32(0)))
        self.rows = rows
        self.split.append(axis)
        return sends[0]

    def turn(self, deps):
        (self.value,) = combine(self.terms, self.rows, [jnp.int32(0)], deps, self.name + "_t")
        self.spread()
        return self.value

    def spread(self):
        if not self.split:
            self.halves = None
            return
        axis = self.split.pop()
        self.gathered = [axis.send(self.value, shift) for shift in range(1, axis.length)]
        self.places = [(axis.place - shift) % axis.length for shift in range(axis.length)]

    def gather(self, deps):
        self.value = self.join(deps)
        self.spread()
        return self.value

    def join(self, deps):
        if self.places is None:
            return self.value
        whole = assemble(
            [self.value] + self.gathered, self.places, deps, "%s_g%d" % (self.name, len(self.split))
        )
        self.places = None
        return whole


def on_device(
    patches,
    pieces,
    ln1_gain,
    ln1_bias,
    qkv_weight,
    qkv_bias,
    out_weight,
    out_bias,
    attn_scale,
    ln2_gain,
    ln2_bias,
    fc1_weight,
    fc1_bias,
    fc2_weight,
    fc2_bias,
    mlp_scale,
    cotangent,
):
    rows, features = patches.shape
    width = out_weight.shape[0]
    hidden_half = fc1_weight.shape[1]
    pairs = width // PAIR
    ext = rows + HALO
    side_index = lax.axis_index("narrow")
    side = side_index.astype(jnp.int32).reshape(1)
    pieces_row = pieces.reshape(-1)
    swap = [(0, 1), (1, 0)]
    axes = wide_axes()

    def other(value):
        return lax.ppermute(value, "narrow", swap)

    halo = other(lax.dynamic_slice_in_dim(patches, (1 - side_index) * (rows - HALO), HALO, 0))
    qkv_bias_par = other(qkv_bias)
    qkv_par = other(qkv_weight)
    out_par = other(out_weight)
    fc1_bias_par = other(fc1_bias)
    fc1_par = other(fc1_weight)
    fc2_par = other(fc2_weight)

    def call(body, name, out_shape, in_specs, flops, nbytes, args, deps=(), scratch=(), grid=None,
             out_specs=None, vmem=56, transcendentals=0):
        count = len(args)
        kept = len(deps)

        def kernel(*refs):
            body(*refs[:count], *refs[count + kept :])

        options = {} if grid is None else {"grid": grid}
        return pl.pallas_call(
            kernel,
            out_shape=out_shape,
            in_specs=list(in_specs) + [ANY] * kept,
            out_specs=out_specs if out_specs is not None else jax.tree.map(lambda _: WHOLE, out_shape),
            scratch_shapes=list(scratch),
            compiler_params=params(vmem),
            cost_estimate=cost(flops, nbytes, transcendentals),
            name=name,
            **options,
        )(*args, *deps)

    qkv_flops = 2 * features * width * (rows + 2 * ext)
    normed1, q_own, k_own, v_own = call(
        first_qkv_kernel, "qkv_own",
        (shape((ext, features), bf16),) + qkv_shapes(rows, width),
        [SCALARS] + [WHOLE] * 6, qkv_flops, 8e6,
        (side, patches, halo, ln1_gain, ln1_bias, qkv_weight, qkv_bias),
    )

    shares_shapes = tuple(shape((pairs, 2 * BLOCK, count), bf16) for _, _, count in unit_table(0))
    area = sum(count for _, _, count in unit_table(0)) * BLOCK * 2 * pairs

    def attend(q, k, v, name):
        return call(
            attend_kernel, name, shares_shapes + (shape((rows, width), bf16),),
            [SCALARS, SCALARS] + [WHOLE] * 3, 4 * area * PAIR, 6e6,
            (side, pieces_row, q, k, v), transcendentals=area,
        )

    *shares_own, att_own = attend(q_own, k_own, v_own, "attend_own")
    q_par, k_par, v_par = call(
        qkv_body, "qkv_par", qkv_shapes(rows, width), [SCALARS] + [WHOLE] * 3, qkv_flops, 6e6,
        (side, normed1, qkv_par, qkv_bias_par), deps=(att_own,),
    )
    *shares_par, att_par = attend(q_par, k_par, v_par, "attend_par")

    steps = 2
    by_row = pl.BlockSpec((rows // steps, features), lambda i: (i, 0))
    att_row = pl.BlockSpec((rows // steps, width), lambda i: (i, 0))
    w_spec = pl.BlockSpec((width, features), lambda i: (0, 0))
    vec = pl.BlockSpec((features,), lambda i: (0,))
    row_f32, row_bf16 = shape((rows, features), f32), shape((rows, features), bf16)
    attn_proj, middle, normed2, grad_mlp = call(
        project_kernel, "project", (row_f32, row_f32, row_bf16, row_bf16),
        [att_row, att_row, w_spec, w_spec, vec, vec, by_row, vec, vec, by_row, vec],
        4 * rows * width * features, 9e6,
        (att_own, att_par, out_weight, out_par, out_bias, attn_scale, patches, ln2_gain, ln2_bias,
         cotangent, mlp_scale),
        grid=(steps,), out_specs=(by_row,) * 4,
    )

    chunks = 2
    per_chunk = hidden_half // chunks
    fb = per_chunk // 2

    def mlp(chunk, deps):
        first = chunk * 2
        const = pl.BlockSpec((rows, features), lambda j: (0, 0))
        w1_spec = pl.BlockSpec((features, fb), lambda j: (0, first + j))
        b1_spec = pl.BlockSpec((1, hidden_half), lambda j: (0, 0))
        w2_spec = pl.BlockSpec((fb, features), lambda j: (first + j, 0))
        pack_spec = pl.BlockSpec((per_chunk + features, features), lambda j: (0, 0))
        db_spec = pl.BlockSpec((1, per_chunk), lambda j: (0, 0))
        pack = shape((per_chunk + features, features), bf16)
        small = shape((1, per_chunk), f32)
        return call(
            partial(mlp_kernel, first_bias=chunk * per_chunk), "mlp_%d" % chunk,
            (pack, pack, small, small, row_f32, row_f32),
            [const, const, w1_spec, w1_spec, b1_spec, b1_spec, w2_spec, w2_spec],
            24 * rows * features * per_chunk, 16e6,
            (normed2, grad_mlp, fc1_weight, fc1_par, fc1_bias.reshape(1, -1),
             fc1_bias_par.reshape(1, -1), fc2_weight, fc2_par),
            deps=deps, grid=(2,),
            out_specs=(pack_spec, pack_spec, db_spec, db_spec, const, const),
            transcendentals=4 * rows * per_chunk,
        )

    pack_own_0, pack_par_0, b1a_own, b1a_par, dn2_0, mlp_out_0 = mlp(0, ())
    group_0 = GroupSum(pack_own_0, other(pack_par_0), axes, "g0")
    pack_own_1, pack_par_1, b1b_own, b1b_par, dn2_1, mlp_out_1 = mlp(1, (pack_par_0,))
    group_1 = GroupSum(pack_own_1, other(pack_par_1), axes, "g1")
    token = group_0.scatter([dn2_1])

    small = shape((1, features), f32)
    (
        grad_middle, ga_own, ga_par, dwo_own, dwo_par, d_gain2, d_bias2, d_attn_scale, d_out_bias,
    ) = call(
        project_back_kernel, "project_back",
        (row_f32, shape((rows, width), bf16), shape((rows, width), bf16),
         shape((features, width), bf16), shape((features, width), bf16), small, small, small, small),
        [WHOLE] * 11, 8 * rows * width * features, 16e6,
        (dn2_0, dn2_1, middle, cotangent, attn_proj, ln2_gain, attn_scale, att_own, att_par,
         out_weight, out_par),
        deps=(token,),
    )

    def attend_back(q, k, v, shares, ga, name, deps):
        return call(
            attend_back_kernel, name,
            (shape((rows, width), bf16), shape((ext, width), bf16), shape((ext, width), bf16)),
            [SCALARS] + [WHOLE] * 8, 8 * area * PAIR, 8e6, (side, q, k, v, *shares, ga), deps=deps,
            scratch=[pltpu.VMEM((pairs, ext, PAIR), f32)] * 2,
        )

    dq_par, dk_par, dv_par = attend_back(
        q_par, k_par, v_par, shares_par, ga_par, "attend_back_par", ()
    )
    token = group_0.scatter([dq_par])
    token = group_1.scatter([token])
    dq_own, dk_own, dv_own = attend_back(
        q_own, k_own, v_own, shares_own, ga_own, "attend_back_own", (token,)
    )
    token = group_0.scatter([dq_own]) if len(axes) > 2 else token

    pack = shape((4 * features, width), bf16)
    qkv_pack_own, qkv_pack_par, qb_own, qb_par, grad_own, grad_halo = call(
        qkv_back_kernel, "qkv_back",
        (pack, pack, shape((2, width), f32), shape((2, width), f32), row_f32,
         shape((HALO, features), bf16)),
        [SCALARS] + [WHOLE] * 11, 4 * qkv_flops, 24e6,
        (side, normed1, dq_own, dk_own, dv_own, dq_par, dk_par, dv_par, qkv_weight, qkv_par, dwo_own,
         dwo_par),
        deps=(token,), scratch=[pltpu.VMEM((ext, features), f32)],
    )
    group_2 = GroupSum(qkv_pack_own, other(qkv_pack_par), axes, "g2")
    halo_back = other(grad_halo)
    token = group_1.scatter([qkv_pack_own])
    while group_0.stage < len(axes):
        token = group_0.scatter([token])
    token = group_0.turn([token])

    grad_patches, d_gain1, d_bias1 = call(
        norm1_back_kernel, "norm1_back", (row_f32, small, small), [SCALARS] + [WHOLE] * 5,
        20 * rows * features, 6e6,
        (side, grad_own, halo_back, patches, ln1_gain, grad_middle), deps=(token,),
        scratch=[pltpu.VMEM((rows, features), f32)],
    )
    token = group_2.scatter([d_gain1])
    vectors = shape((VECTOR_ROWS, features), f32)
    output, mine, theirs = call(
        finish_kernel, "finish", (row_bf16, vectors, vectors), [WHOLE] * 19,
        20 * rows * features, 8e6,
        (mlp_out_0, mlp_out_1, middle, cotangent, grad_mlp, fc2_bias, mlp_scale, d_gain1, d_bias1,
         d_gain2, d_bias2, d_attn_scale, d_out_bias, qb_own, qb_par, b1a_own, b1a_par, b1b_own,
         b1b_par),
        deps=(token,),
    )
    vector_terms = [mine, other(theirs)]

    def add_vectors(deps):
        return call(
            partial(add_kernel, terms=len(vector_terms)), "add_vectors", vectors,
            [WHOLE] * len(vector_terms), 1e5, 2e5, vector_terms, deps=deps,
        )

    token = mine
    pending = [group_1, group_0, group_2]
    vector_axes = list(axes)
    while any(g.stage < len(axes) for g in pending) or vector_axes:
        for group in (group_1, group_2):
            if group.stage < len(axes):
                token = group.scatter([token])
        if vector_axes:
            axis = vector_axes.pop(0)
            total = add_vectors([token])
            vector_terms = [total] + [axis.send(total, s) for s in range(1, axis.length)]
            token = total
        if group_0.split:
            token = group_0.gather([token])
    token = group_1.turn([token])
    token = group_2.turn([token])
    while group_0.split or group_1.split or group_2.split:
        for group in (group_0, group_1, group_2):
            if group.split:
                token = group.gather([token])
    results = [group.join([token]) for group in (group_0, group_1, group_2)]

    one = shape((features,), f32)
    (
        d_gain1, d_bias1, d_gain2, d_bias2, d_attn_scale, d_out_bias, d_mlp_scale, d_fc2_bias,
        grad_qkv_bias, grad_fc1_bias,
    ) = call(
        partial(unpack_kernel, terms=len(vector_terms), deps=0), "unpack",
        (one,) * 8 + (shape((2, width), f32), shape((hidden_half,), f32)),
        [WHOLE] * len(vector_terms), 1e5, 2e5, vector_terms, deps=(token,),
    )

    fc_0, fc_1, qkv = results
    grad_fc2_weight = jnp.concatenate([fc_0[:per_chunk], fc_1[:per_chunk]], axis=0).astype(f32)
    grad_fc1_weight = jnp.concatenate([fc_0[per_chunk:], fc_1[per_chunk:]], axis=1).astype(f32)
    grad_qkv_weight = qkv[: 3 * features].astype(f32).reshape(3, features, width)
    tail = qkv[3 * features :].astype(f32)
    grad_out_weight = jnp.concatenate(
        [tail[part * width : (part + 1) * width] for part in range(features // width)], axis=1
    )
    return (
        output,
        grad_patches,
        d_gain1,
        d_bias1,
        grad_qkv_weight,
        grad_qkv_bias,
        grad_out_weight,
        d_out_bias,
        d_attn_scale,
        d_gain2,
        d_bias2,
        grad_fc1_weight,
        grad_fc1_bias,
        grad_fc2_weight,
        d_fc2_bias,
        d_mlp_scale,
    )


def solution(mesh):
    in_specs = (
        P(("wide", "narrow"), None),
        P("wide", None),
        P(),
        P(),
        P(None, None, "narrow"),
        P(None, "narrow"),
        P("narrow", None),
        P(),
        P(),
        P(),
        P(),
        P(None, "narrow"),
        P("narrow"),
        P("narrow", None),
        P(),
        P(),
        P(("wide", "narrow"), None),
    )
    out_specs = (
        P(("wide", "narrow"), None),
        P(("wide", "narrow"), None),
        P(),
        P(),
        P(None, None, "narrow"),
        P(None, "narrow"),
        P("narrow", None),
        P(),
        P(),
        P(),
        P(),
        P(None, "narrow"),
        P("narrow"),
        P("narrow", None),
        P(),
        P(),
    )
    return jax.shard_map(
        on_device, mesh=mesh, in_specs=in_specs, out_specs=out_specs, check_vma=False
    )
```

```python
from functools import partial
import math

import jax
import jax.numpy as jnp
from jax import lax
from jax.sharding import PartitionSpec as P
from jax.experimental import pallas as pl
from jax.experimental.pallas import tpu as pltpu

HEAD = 64
PAIR = 2 * HEAD
HALO = 256
BLOCK = 128

epsilon = 1e-06
masked_score = -1e30

bf16 = jnp.bfloat16
f32 = jnp.float32

WHOLE = pl.BlockSpec(memory_space=pltpu.VMEM)
SCALARS = pl.BlockSpec(memory_space=pltpu.SMEM)
ANY = pl.BlockSpec(memory_space=pl.ANY)
FAR = pl.BlockSpec(memory_space=pltpu.HBM)


def params(mib):
    return pltpu.CompilerParams(vmem_limit_bytes=mib * 1024 * 1024)


COST_SCALE = 10.0


def cost(flops, nbytes, transcendentals=0):
    return pl.CostEstimate(
        flops=int(flops * COST_SCALE),
        bytes_accessed=int(nbytes * COST_SCALE),
        transcendentals=int(transcendentals * COST_SCALE),
    )


def shape(dims, dtype):
    return jax.ShapeDtypeStruct(dims, dtype)


def dot(a, b):
    return jnp.dot(a, b, preferred_element_type=f32)


def dot_bt(a, b):
    return lax.dot_general(a, b, (((1,), (1,)), ((), ())), preferred_element_type=f32)


def dot_at(a, b):
    return lax.dot_general(a, b, (((0,), (0,)), ((), ())), preferred_element_type=f32)


def row_stats(values):
    average = jnp.mean(values, axis=-1, keepdims=True)
    centred = values - average
    inverse = lax.rsqrt(jnp.mean(centred * centred, axis=-1, keepdims=True) + epsilon)
    return centred * inverse, inverse


def norm_back(upstream, normed, inverse, gain):
    scaled = upstream * gain
    centred = scaled - jnp.mean(scaled, axis=-1, keepdims=True)
    centred = centred - normed * jnp.mean(scaled * normed, axis=-1, keepdims=True)
    return centred * inverse


def flat(vector):
    return vector[...].reshape(1, -1)


def column_sum(values):
    return jnp.sum(values, axis=0, keepdims=True)


def norm1_body(side, patches, halo, gain, bias, normed):
    rows = patches.shape[0]
    side_index = side[0]
    own_start = pl.multiple_of(side_index * HALO, HALO)
    halo_start = pl.multiple_of((1 - side_index) * rows, HALO)
    step = 128
    for source, start in ((patches, own_start), (halo, halo_start)):
        for first in range(0, source.shape[0], step):
            xhat, _ = row_stats(source[first : first + step, :].astype(f32))
            normed[pl.ds(start + first, step), :] = (xhat * flat(gain) + flat(bias)).astype(bf16)


def qkv_body(side, normed, weight, bias, queries, keys, values):
    pairs, rows, _ = queries.shape
    own_start = pl.multiple_of(side[0] * HALO, HALO)
    factor = 1.0 / math.sqrt(HEAD)
    ext = normed[...]
    own = normed[pl.ds(own_start, rows), :]
    query = (dot(own, weight[0]) + bias[0:1, :]).astype(bf16).astype(f32) * factor
    key = dot(ext, weight[1])
    value = dot(ext, weight[2]) + bias[1:2, :]
    for full, target in ((query, queries), (key, keys), (value, values)):
        for pair in range(pairs):
            target[pair] = full[:, pair * PAIR : (pair + 1) * PAIR].astype(bf16)


def unit_table(side_index):
    return (
        ((2 - 2 * side_index) * BLOCK, 0, 5 * BLOCK),
        ((3 - 2 * side_index) * BLOCK, BLOCK, 5 * BLOCK),
        ((1 + side_index) * BLOCK, 2 * side_index * BLOCK, 4 * BLOCK),
        (3 * side_index * BLOCK, 3 * side_index * BLOCK, 3 * BLOCK),
    )


def aligned(value):
    if isinstance(value, int):
        return value
    return pl.multiple_of(value, BLOCK)


def pair_stack(block):
    lane = lax.broadcasted_iota(jnp.int32, block.shape, 1)
    zero = jnp.zeros_like(block)
    return jnp.concatenate(
        [jnp.where(lane < HEAD, block, zero), jnp.where(lane >= HEAD, block, zero)], axis=0
    )


def pair_merge(stacked):
    half = stacked.shape[0] // 2
    lane = lax.broadcasted_iota(jnp.int32, (half, stacked.shape[1]), 1)
    return jnp.where(lane < HEAD, stacked[:half], stacked[half:])


def mask_bias(side_index, pieces, images, first_query, first_key, key_count):
    base = side_index * HALO
    place = lax.broadcasted_iota(jnp.int32, (BLOCK, 1), 0) + (first_query + 2 * base)
    start = jnp.zeros_like(place)
    end = jnp.full_like(place, 2**30)
    running = jnp.int32(0)
    for image in range(images):
        running = running + pieces[image]
        start = jnp.where(place >= running, running, start)
        end = jnp.where(place < running, jnp.minimum(end, running), end)
    padding = place >= running
    start = jnp.where(padding, place, start)
    end = jnp.where(padding, place + 1, end)
    key_place = lax.broadcasted_iota(jnp.int32, (BLOCK, key_count), 1) + (first_key + base)
    return jnp.where((key_place >= start) & (key_place < end), 0.0, masked_score).astype(f32)


class Copies:
    def __init__(self, semaphores):
        self.semaphores = semaphores
        self.count = 0
        self.leaving = []

    def start(self, source, target):
        copy = pltpu.make_async_copy(source, target, self.semaphores.at[self.count])
        self.count += 1
        copy.start()
        return copy

    def fetch(self, *pairs):
        return [self.start(source, target) for source, target in pairs]

    def put(self, source, target):
        self.leaving.append(self.start(source, target))

    def finish(self):
        for copy in self.leaving:
            copy.wait()


def arrived(copies):
    for copy in copies:
        copy.wait()


def attend_all(side, pieces, biases, queries, keys, values, shares_refs, shares_out, attended, copies):
    side_index = side[0]

    def one_pair(pair, carry):
        columns = pl.ds(pl.multiple_of(pair * PAIR, PAIR), PAIR)
        for (first_query, first_key, count), bias, shares_ref in zip(
            unit_table(side_index), biases, shares_refs
        ):
            query_rows = pl.ds(aligned(first_query), BLOCK)
            key_rows = pl.ds(aligned(first_key), count)
            stacked = pair_stack(queries[pair, query_rows, :])
            scores = dot_bt(stacked, keys[pair, key_rows, :])
            scores = (scores.reshape(2, BLOCK, count) + bias[...][None]).reshape(2 * BLOCK, count)
            weights = jnp.exp(scores - jnp.max(scores, axis=-1, keepdims=True))
            total = jnp.sum(weights, axis=-1, keepdims=True)
            shares = (weights * (1.0 / total)).astype(bf16)
            shares_ref[pair] = shares
            merged = pair_merge(dot(shares, values[pair, key_rows, :]))
            attended[query_rows, columns] = merged.astype(bf16)
        return carry

    lax.fori_loop(0, queries.shape[0], one_pair, 0)
    for shares_ref, out in zip(shares_refs, shares_out):
        copies.put(shares_ref, out)


def make_biases(side, pieces, biases):
    for (first_query, first_key, count), bias in zip(unit_table(side[0]), biases):
        bias[...] = mask_bias(side[0], pieces, pieces.shape[0] - 1, first_query, first_key, count)


def attend_first_kernel(
    side, pieces, gain, bias, qbias, patches_in, halo_in, weight_in,
    normed_out, q_out, k_out, v_out, p0_out, p1_out, p2_out, p3_out, att_out,
    patches, halo, weight, normed, queries, keys, values, p0, p1, p2, p3, attended,
    b0, b1, b2, b3, semaphores,
):
    copies = Copies(semaphores)
    rows = copies.fetch((patches_in, patches), (halo_in, halo))
    weights = copies.fetch((weight_in, weight))
    biases = (b0, b1, b2, b3)
    make_biases(side, pieces, biases)
    arrived(rows)
    norm1_body(side, patches, halo, gain, bias, normed)
    copies.put(normed, normed_out)
    arrived(weights)
    qkv_body(side, normed, weight, qbias, queries, keys, values)
    copies.put(queries, q_out)
    copies.put(keys, k_out)
    copies.put(values, v_out)
    attend_all(
        side, pieces, biases, queries, keys, values, (p0, p1, p2, p3),
        (p0_out, p1_out, p2_out, p3_out), attended, copies,
    )
    copies.put(attended, att_out)
    copies.finish()


def attend_second_kernel(
    side, pieces, qbias, out_bias, scale, gain, bias,
    normed_in, weight_in, att_own_in, w_own_in, w_par_in, patches_in,
    q_out, k_out, v_out, p0_out, p1_out, p2_out, p3_out, att_out, middle_out, normed2,
    normed, weight, att_own, w_own, w_par, patches, queries, keys, values, p0, p1, p2, p3,
    attended, b0, b1, b2, b3, middle, semaphores,
):
    copies = Copies(semaphores)
    first = copies.fetch((normed_in, normed), (weight_in, weight))
    later = copies.fetch(
        (att_own_in, att_own), (w_own_in, w_own), (w_par_in, w_par), (patches_in, patches)
    )
    biases = (b0, b1, b2, b3)
    make_biases(side, pieces, biases)
    arrived(first)
    qkv_body(side, normed, weight, qbias, queries, keys, values)
    copies.put(queries, q_out)
    copies.put(keys, k_out)
    copies.put(values, v_out)
    attend_all(
        side, pieces, biases, queries, keys, values, (p0, p1, p2, p3),
        (p0_out, p1_out, p2_out, p3_out), attended, copies,
    )
    copies.put(attended, att_out)
    arrived(later)
    half = patches.shape[0] // 2
    for start in range(0, 2 * half, half):
        block = slice(start, start + half)
        proj = dot(att_own[block, :], w_own[...]) + dot(attended[block, :], w_par[...]) + flat(out_bias)
        mid = patches[block, :].astype(f32) + flat(scale) * proj
        middle[block, :] = mid
        copies.put(middle.at[block], middle_out.at[block])
        xhat, _ = row_stats(mid)
        normed2[block, :] = (xhat * flat(gain) + flat(bias)).astype(bf16)
    copies.finish()


def attend_back_body(side, queries, keys, values, shares_refs, shares_copies, upstream, dq, dk, dv, acc_k, acc_v):
    side_index = side[0]
    factor = 1.0 / math.sqrt(HEAD)
    arrived(shares_copies)

    def one_pair(pair, carry):
        columns = pl.ds(pl.multiple_of(pair * PAIR, PAIR), PAIR)
        acc_k[...] = jnp.zeros_like(acc_k)
        acc_v[...] = jnp.zeros_like(acc_v)
        for (first_query, first_key, count), shares_ref in zip(unit_table(side_index), shares_refs):
            query_rows = pl.ds(aligned(first_query), BLOCK)
            key_rows = pl.ds(aligned(first_key), count)
            stacked_q = pair_stack(queries[pair, query_rows, :])
            stacked_g = pair_stack(upstream[query_rows, columns])
            shares = shares_ref[pair]
            wide_shares = shares.astype(f32)
            grad_shares = dot_bt(stacked_g, values[pair, key_rows, :])
            inner = jnp.sum(wide_shares * grad_shares, axis=-1, keepdims=True)
            grad_scores = (wide_shares * (grad_shares - inner)).astype(bf16)
            merged = pair_merge(dot(grad_scores, keys[pair, key_rows, :])) * factor
            dq[query_rows, columns] = merged.astype(bf16)
            acc_k[key_rows, :] += dot_at(grad_scores, stacked_q)
            acc_v[key_rows, :] += dot_at(shares, stacked_g)
        dk[:, columns] = acc_k[...].astype(bf16)
        dv[:, columns] = acc_v[...].astype(bf16)
        return carry

    lax.fori_loop(0, queries.shape[0], one_pair, 0)


def attend_back_kernel(
    side, upstream, dwo, before, q_in, k_in, v_in, p0_in, p1_in, p2_in, p3_in, normed_in, weight_in,
    pack, bias, total, grad_own_out, grad_halo,
    queries, keys, values, p0, p1, p2, p3, normed, weight, dq, dk, dv, acc_k, acc_v, grad_own,
    semaphores,
):
    copies = Copies(semaphores)
    shares = (p0, p1, p2, p3)
    first = copies.fetch((v_in, values), (k_in, keys), (q_in, queries))
    share_copies = copies.fetch(*zip((p0_in, p1_in, p2_in, p3_in), shares))
    later = copies.fetch((normed_in, normed), (weight_in, weight))
    arrived(first)
    attend_back_body(
        side, queries, keys, values, shares, share_copies, upstream, dq, dk, dv, acc_k, acc_v
    )
    arrived(later)
    features = normed.shape[1]
    rows = dq.shape[0]
    own_rows = pl.ds(pl.multiple_of(side[0] * HALO, HALO), rows)
    halo_rows = pl.ds(pl.multiple_of((1 - side[0]) * rows, HALO), HALO)
    for index, (left, right) in enumerate(
        ((normed[own_rows, :], dq), (normed[...], dk), (normed[...], dv))
    ):
        pack[index * features : (index + 1) * features, :] = dot_at(left, right[...]).astype(bf16)
    pack[3 * features : 4 * features, :] = dwo[...]
    bias[0:1, :] = column_sum(dq[...].astype(f32))
    bias[1:2, :] = column_sum(dv[...].astype(f32))
    added = dot_bt(dk[...], weight[1]) + dot_bt(dv[...], weight[2])
    own_added = dot_bt(dq[...], weight[0])
    if before is None:
        total[...] = added
        total[own_rows, :] += own_added
    else:
        total[...] = before[...] + added
        grad_own[...] = total[own_rows, :] + own_added
        grad_halo[...] = total[halo_rows, :].astype(bf16)
        copies.put(grad_own, grad_own_out)
    copies.finish()


def mlp_kernel(mlp_scale, b1, normed2, cotangent, w1, w2, hidden_out, pack, gb, db, grad_mlp, bias_row):
    chunk = pl.program_id(0)

    @pl.when(chunk == 0)
    def _():
        grad_mlp[...] = (cotangent[...].astype(f32) * flat(mlp_scale)).astype(bf16)
        bias_row[...] = flat(b1)

    columns = w1.shape[1]
    n2 = normed2[...]
    gm = grad_mlp[...]
    bias = bias_row[:, pl.ds(pl.multiple_of(chunk * columns, columns), columns)]
    before = dot(n2, w1[...]) + bias
    grad_hidden = dot_bt(gm, w2[...])
    below = 0.5 + 0.5 * lax.erf(before * math.sqrt(0.5))
    density = jnp.exp(before * before * -0.5) * (1.0 / math.sqrt(2.0 * math.pi))
    hidden = (before * below).astype(bf16)
    hidden_out[0] = hidden
    pack[0, 0] = dot_at(hidden, gm).astype(bf16)
    grad_before = (grad_hidden * (below + before * density)).astype(bf16)
    gb[0] = grad_before
    db[0] = column_sum(grad_before.astype(f32))
    pack[0, 1] = dot_at(grad_before, n2).astype(bf16)


def project_back_kernel(
    gain, scale, gb_own, gb_par, w1_own_in, w1_par_in,
    middle_in, patches_in, cotangent_in, att_own_in, att_par_in, w_own_in, w_par_in,
    grad_middle_out, ga_own, ga_par, dwo_own, dwo_par, d_gain, d_bias, d_scale, d_out_bias,
    w1_own, w1_par, middle, patches, cotangent, att_own, att_par, w_own, w_par, grad_middle,
    semaphores,
):
    copies = Copies(semaphores)
    first = copies.fetch((w1_own_in, w1_own))
    second = copies.fetch((w1_par_in, w1_par))
    later = copies.fetch(
        (middle_in, middle), (cotangent_in, cotangent), (patches_in, patches),
        (w_own_in, w_own), (w_par_in, w_par), (att_own_in, att_own), (att_par_in, att_par),
    )
    chunk = gb_own.shape[2]
    arrived(first)
    upstream = dot_bt(gb_own[0], w1_own[:, :chunk]) + dot_bt(gb_own[1], w1_own[:, chunk:])
    arrived(second)
    upstream += dot_bt(gb_par[0], w1_par[:, :chunk]) + dot_bt(gb_par[1], w1_par[:, chunk:])
    arrived(later)
    mid = middle[...]
    xhat, inverse = row_stats(mid)
    d_gain[...] = column_sum(upstream * xhat)
    d_bias[...] = column_sum(upstream)
    grad_mid = cotangent[...].astype(f32) + norm_back(upstream, xhat, inverse, flat(gain))
    grad_middle[...] = grad_mid
    d_scale[...] = column_sum(grad_mid * (mid - patches[...].astype(f32))) / flat(scale)
    grad_proj = (grad_mid * flat(scale)).astype(bf16)
    d_out_bias[...] = column_sum(grad_proj.astype(f32))
    width = att_own.shape[1]
    for att, weight, ga, dwo in ((att_par, w_par, ga_par, dwo_par), (att_own, w_own, ga_own, dwo_own)):
        ga[...] = dot_bt(grad_proj, weight[...]).astype(bf16)
        full = dot_at(att[...], grad_proj).astype(bf16)
        for part in range(full.shape[1] // width):
            columns = slice(part * width, (part + 1) * width)
            dwo[columns, :] = full[:, columns]
    copies.put(grad_middle, grad_middle_out)
    copies.finish()


def norm1_back_kernel(side, grad_own, grad_halo, patches, gain, grad_middle, out, d_gain, d_bias, total):
    start = pl.multiple_of((1 - side[0]) * (grad_own.shape[0] - HALO), HALO)
    total[...] = grad_own[...]
    total[pl.ds(start, HALO), :] += grad_halo[...].astype(f32)
    upstream = total[...]
    xhat, inverse = row_stats(patches[...].astype(f32))
    d_gain[...] = column_sum(upstream * xhat)
    d_bias[...] = column_sum(upstream)
    out[...] = grad_middle[...] + norm_back(upstream, xhat, inverse, flat(gain))


VECTOR_ROWS = 16
PREP_MIB = 24
VMEM_ATTEND = 22
VMEM_MLP = 32
VMEM_BACK = 26


def finish_kernel(
    h_own, h_par, w2_own, w2_par, middle, cotangent, fc2_bias, scale,
    d_gain1, d_bias1, d_gain2, d_bias2, d_attn_scale, d_out_bias, qb_own, qb_par,
    b1_own, b1_par,
    out, mine, theirs,
):
    features = middle.shape[1]
    chunk = h_own.shape[2]
    mlp_out = flat(fc2_bias) + (
        dot(h_own[0], w2_own[0:chunk, :])
        + dot(h_own[1], w2_own[chunk:, :])
        + dot(h_par[0], w2_par[0:chunk, :])
        + dot(h_par[1], w2_par[chunk:, :])
    )
    out[...] = (middle[...] + flat(scale) * mlp_out).astype(bf16)
    upstream = cotangent[...].astype(f32)
    d_scale = column_sum(upstream * mlp_out)
    d_bias = column_sum((upstream * flat(scale)).astype(bf16).astype(f32))
    width = qb_own.shape[1]
    for pack, qb, b1 in ((mine, qb_own, b1_own), (theirs, qb_par, b1_par)):
        pack[...] = jnp.zeros_like(pack)
        for index, vector in enumerate((d_gain1, d_bias1, d_gain2, d_bias2, d_attn_scale, d_out_bias)):
            pack[index : index + 1, :] = vector[...]
        pack[6:7, :] = d_scale
        pack[7:8, :] = d_bias
        pack[8:9, 0:width] = qb[0:1, :]
        pack[9:10, 0:width] = qb[1:2, :]
        pack[10:11, :] = b1[0]
        pack[11:12, :] = b1[1]


def unpack_kernel(
    *refs, terms, deps
):
    total = refs[0][...]
    for index in range(1, terms):
        total = total + refs[index][...]
    (
        d_gain1, d_bias1, d_gain2, d_bias2, d_attn_scale, d_out_bias, d_scale, d_bias, qb, b1,
    ) = refs[terms + deps :]
    for index, out in enumerate(
        (d_gain1, d_bias1, d_gain2, d_bias2, d_attn_scale, d_out_bias, d_scale, d_bias)
    ):
        out[...] = total[index]
    width = qb.shape[1]
    qb[0:1, :] = total[8:9, 0:width]
    qb[1:2, :] = total[9:10, 0:width]
    half = b1.shape[0] // 2
    b1[0:half] = total[10]
    b1[half:] = total[11]


def add_kernel(*refs, terms):
    total = refs[0][...]
    for index in range(1, terms):
        total = total + refs[index][...]
    refs[-1][...] = total


def wide_factors(size):
    lengths = []
    rest = size
    while rest % 4 == 0 and rest > 4:
        lengths.append(4)
        rest //= 4
    if rest == 4:
        lengths += [2, 2]
    elif rest > 1:
        lengths.append(rest)
    factors = []
    stride = size
    for length in lengths:
        stride //= length
        factors.append((length, stride))
    return factors[::-1]


def place_in(factor):
    length, stride = factor
    return (lax.axis_index("wide") // stride) % length


class Axis:
    def __init__(self, even, odd):
        self.even, self.odd = even, odd
        self.length = even[0]
        side = lax.axis_index("narrow")
        self.place = jnp.where(side == 0, place_in(even), place_in(odd)).astype(jnp.int32)

    def send(self, value, shift):
        pairs = []
        groups = lax.axis_size("narrow")
        for index in range(lax.axis_size("wide")):
            for side in range(groups):
                length, stride = self.odd if side else self.even
                here = (index // stride) % length
                target = index + ((here + shift) % length - here) * stride
                pairs.append((index * groups + side, target * groups + side))
        return lax.ppermute(value, ("wide", "narrow"), pairs)


def wide_axes():
    factors = wide_factors(lax.axis_size("wide"))
    if len(factors) > 1 and factors[0][0] == factors[1][0]:
        first, second = factors[:2]
        return [Axis(first, second), Axis(second, first)] + [Axis(f, f) for f in factors[2:]]
    return [Axis(f, f) for f in factors]


def combine_kernel(starts, *refs, terms, outs, deps):
    for out in range(outs):
        total = refs[out * terms][...].astype(f32)
        for term in range(1, terms):
            total = total + refs[out * terms + term][...].astype(f32)
        refs[outs * terms + deps + out][...] = total.astype(bf16)


def combine(terms, rows, blocks, deps, name):
    columns = terms[0].shape[1]
    tile = rows
    while tile * columns > 384 * 768 and tile % 32 == 0:
        tile //= 2
    starts = jnp.stack([(block * (rows // tile)).astype(jnp.int32) for block in blocks])
    out_spec = pl.BlockSpec((tile, columns), lambda g, s: (g, 0))
    return pl.pallas_call(
        partial(combine_kernel, terms=len(terms), outs=len(blocks), deps=len(deps)),
        out_shape=[shape((rows, columns), bf16)] * len(blocks),
        grid_spec=pltpu.PrefetchScalarGridSpec(
            num_scalar_prefetch=1,
            grid=(rows // tile,),
            in_specs=[
                pl.BlockSpec((tile, columns), lambda g, s, i=i: (s[i] + g, 0))
                for i in range(len(blocks))
                for _ in terms
            ]
            + [ANY] * len(deps),
            out_specs=[out_spec] * len(blocks),
        ),
        compiler_params=params(PREP_MIB),
        cost_estimate=cost(rows * columns, rows * columns),
        name=name,
    )(starts, *[term for _ in blocks for term in terms], *deps)


def assemble_kernel(starts, *refs, count, deps):
    out = refs[count + deps]
    rows = refs[0].shape[0]
    for index in range(count):
        out[pl.ds(pl.multiple_of(starts[index], 16), rows), :] = refs[index][...]


def assemble(blocks, places, deps, name):
    rows, columns = blocks[0].shape
    starts = jnp.stack([(place * rows).astype(jnp.int32) for place in places])
    return pl.pallas_call(
        partial(assemble_kernel, count=len(blocks), deps=len(deps)),
        out_shape=shape((rows * len(blocks), columns), bf16),
        in_specs=[SCALARS] + [WHOLE] * len(blocks) + [ANY] * len(deps),
        out_specs=WHOLE,
        compiler_params=params(PREP_MIB),
        cost_estimate=cost(rows * columns, rows * columns),
        name=name,
    )(starts, *blocks, *deps)


class GroupSum:
    def __init__(self, own, received, axes, name):
        self.terms = [own, received]
        self.axes = axes
        self.name = name
        self.stage = 0
        self.split = []

    def scatter(self, deps):
        axis = self.axes[self.stage]
        name = "%s_s%d" % (self.name, self.stage)
        self.stage += 1
        length = axis.length
        whole = self.terms[0].shape[0]
        rows = whole // length
        if whole % length or rows % 16:
            (total,) = combine(self.terms, whole, [jnp.int32(0)], deps, name)
            self.terms = [total] + [axis.send(total, shift) for shift in range(1, length)]
            return total
        blocks = [(axis.place + shift) % length for shift in range(length)]
        keep, *sends = combine(self.terms, rows, blocks, deps, name)
        self.terms = [keep] + [axis.send(block, shift) for shift, block in enumerate(sends, 1)]
        self.split.append(axis)
        return keep

    def turn(self, deps):
        value = self.terms[0]
        if len(self.terms) > 1:
            (value,) = combine(
                self.terms, value.shape[0], [jnp.int32(0)], deps, self.name + "_t"
            )
        self.spread(value)
        return value

    def spread(self, value):
        self.parts, self.places = [value], [jnp.int32(0)]
        if self.split:
            axis = self.split.pop()
            self.parts = [value] + [axis.send(value, shift) for shift in range(1, axis.length)]
            self.places = [(axis.place - shift) % axis.length for shift in range(axis.length)]

    def gather(self, deps):
        value = self.join(deps)
        self.spread(value)
        return value

    def join(self, deps):
        if len(self.parts) == 1:
            return self.parts[0]
        return assemble(
            self.parts, self.places, deps, "%s_g%d" % (self.name, len(self.split))
        )


def pick(place, mine, received):
    own_first = place == 0
    first = jnp.where(own_first, mine, received)
    second = jnp.where(own_first, received, mine)
    return first.astype(f32), second.astype(f32)


def unpack_fc_kernel(place, mine, received, *refs):
    first, second = pick(place[0], mine[...], received[...])
    refs[-2][...] = first
    refs[-1][...] = second.T


def unpack_fc(group, chunk, chunks, previous, deps, name):
    mine, received = group.parts
    rows, columns = mine.shape
    tile = rows // 3
    part = pl.BlockSpec((tile, columns), lambda g: (g, 0))
    return pl.pallas_call(
        unpack_fc_kernel,
        grid=(3,),
        out_shape=(shape((rows * chunks, columns), f32), shape((rows, columns * chunks), f32)),
        in_specs=[SCALARS, part, part] + [ANY] * (len(previous) + len(deps)),
        out_specs=(
            pl.BlockSpec((tile, columns), lambda g: (3 * chunk + g, 0)),
            pl.BlockSpec((columns, tile), lambda g: (0, 3 * chunk + g)),
        ),
        input_output_aliases={3 + index: index for index in range(len(previous))},
        compiler_params=params(PREP_MIB),
        cost_estimate=cost(rows * columns, rows * columns),
        name=name,
    )(group.places[0].reshape(1), mine, received, *previous, *deps)


def unpack_qkv_kernel(place, mine, received, *refs):
    qkv, out = refs[-2:]
    first, second = pick(place[0], mine[...], received[...])
    features, width = qkv.shape[1:]
    qkv[0] = first[:features]
    qkv[1] = first[features:]
    qkv[2] = second[:features]
    for part in range(features // width):
        columns = slice(part * width, (part + 1) * width)
        out[:, columns] = second[features + part * width : features + (part + 1) * width]


def unpack_qkv(group, deps, name):
    mine, received = group.parts
    rows, width = mine.shape
    features = rows // 2
    return pl.pallas_call(
        unpack_qkv_kernel,
        out_shape=(shape((3, features, width), f32), shape((width, features), f32)),
        in_specs=[SCALARS, WHOLE, WHOLE] + [ANY] * len(deps),
        out_specs=(WHOLE, WHOLE),
        compiler_params=params(PREP_MIB),
        cost_estimate=cost(rows * width, rows * width),
        name=name,
    )(group.places[0].reshape(1), mine, received, *deps)


def on_device(
    patches,
    pieces,
    ln1_gain,
    ln1_bias,
    qkv_weight,
    qkv_bias,
    out_weight,
    out_bias,
    attn_scale,
    ln2_gain,
    ln2_bias,
    fc1_weight,
    fc1_bias,
    fc2_weight,
    fc2_bias,
    mlp_scale,
    cotangent,
):
    rows, features = patches.shape
    width = out_weight.shape[0]
    hidden_half = fc1_weight.shape[1]
    pairs = width // PAIR
    ext = rows + HALO
    side_index = lax.axis_index("narrow")
    side = side_index.astype(jnp.int32).reshape(1)
    pieces_row = pieces.reshape(-1)
    swap = [(0, 1), (1, 0)]
    axes = wide_axes()

    def other(value):
        return lax.ppermute(value, "narrow", swap)

    halo = other(lax.dynamic_slice_in_dim(patches, (1 - side_index) * (rows - HALO), HALO, 0))
    qkv_par = other(qkv_weight)
    qkv_bias_par = other(qkv_bias)
    out_par = other(out_weight)
    fc1_bias_par = other(fc1_bias)
    fc1_par = other(fc1_weight)
    fc2_par = other(fc2_weight)

    def call(body, name, out_shape, in_specs, flops, nbytes, args, deps=(), scratch=(), grid=None,
             out_specs=None, vmem=56, transcendentals=0):
        count = len(args)
        kept = len(deps)

        def kernel(*refs):
            body(*refs[:count], *refs[count + kept :])

        options = {} if grid is None else {"grid": grid}
        return pl.pallas_call(
            kernel,
            out_shape=out_shape,
            in_specs=list(in_specs) + [ANY] * kept,
            out_specs=out_specs if out_specs is not None else jax.tree.map(lambda _: WHOLE, out_shape),
            scratch_shapes=list(scratch),
            compiler_params=params(vmem),
            cost_estimate=cost(flops, nbytes, transcendentals),
            name=name,
            **options,
        )(*args, *deps)

    def fixed(*dims):
        return pl.BlockSpec(dims, lambda *_: (0,) * len(dims))

    counts = [count for _, _, count in unit_table(0)]
    area = sum(counts) * BLOCK * 2 * pairs
    qkv_flops = 2 * features * width * (rows + 2 * ext)
    row_f32, row_bf16 = shape((rows, features), f32), shape((rows, features), bf16)
    att_shape = shape((rows, width), bf16)
    ext_bf16, ext_f32 = shape((ext, features), bf16), shape((ext, features), f32)
    weight_shape = shape((3, features, width), bf16)
    w_shape = shape((width, features), bf16)
    halo_shape = shape((HALO, features), bf16)
    head_shapes = [shape((pairs, n, PAIR), bf16) for n in (rows, ext, ext)]
    share_shapes = [shape((pairs, 2 * BLOCK, count), bf16) for count in counts]
    bias_shapes = [shape((BLOCK, count), f32) for count in counts]

    def staged(body, name, near, far, far_outs, near_outs, scratch, flops, vmem, deps=(),
               transcendentals=0):
        far_shapes = tuple(pltpu.HBM(item.shape, item.dtype) for item in far_outs)
        far = [pltpu.with_memory_space_constraint(arg, pltpu.HBM) for arg in far]
        near = [
            arg if arg.ndim > 1 or arg.dtype == jnp.int32
            else pltpu.with_memory_space_constraint(arg, pltpu.HBM)
            for arg in near
        ]
        return call(
            body, name, far_shapes + tuple(near_outs),
            [SCALARS if arg.dtype == jnp.int32 else WHOLE for arg in near] + [FAR] * len(far),
            flops, 1e7, tuple(near) + tuple(far), deps=deps,
            out_specs=(FAR,) * len(far_outs) + (WHOLE,) * len(near_outs),
            scratch=[pltpu.VMEM(item.shape, item.dtype) for item in scratch]
            + [pltpu.SemaphoreType.DMA((len(far) + len(far_outs) + 8,))],
            transcendentals=transcendentals, vmem=vmem,
        )

    normed1, *heads_own, att_own = staged(
        attend_first_kernel, "attend_own",
        (side, pieces_row, ln1_gain, ln1_bias, qkv_bias), (patches, halo, qkv_weight),
        [ext_bf16] + head_shapes + share_shapes + [att_shape], (),
        [row_bf16, halo_shape, weight_shape, ext_bf16] + head_shapes + share_shapes + [att_shape]
        + bias_shapes,
        4 * area * PAIR + qkv_flops, VMEM_ATTEND, transcendentals=area,
    )
    *heads_par, att_par, middle, normed2 = staged(
        attend_second_kernel, "attend_par",
        (side, pieces_row, qkv_bias_par, out_bias, attn_scale, ln2_gain, ln2_bias),
        (normed1, qkv_par, att_own, out_weight, out_par, patches),
        head_shapes + share_shapes + [att_shape, row_f32], (row_bf16,),
        [ext_bf16, weight_shape, att_shape, w_shape, w_shape, row_bf16] + head_shapes + share_shapes
        + [att_shape] + bias_shapes + [row_f32],
        4 * area * PAIR + qkv_flops + 4 * rows * width * features, VMEM_ATTEND + 6,
        transcendentals=area,
    )

    chunks = 2
    per_chunk = hidden_half // chunks
    w1_shape = shape((features, hidden_half), bf16)

    def mlp(w1, b1, w2, name, deps=()):
        part = pl.BlockSpec((1, rows, per_chunk), lambda j: (j, 0, 0))
        w1, w2, b1, scale = [
            pltpu.with_memory_space_constraint(arg, pltpu.HBM) for arg in (w1, w2, b1, mlp_scale)
        ]
        return call(
            mlp_kernel, name,
            (pltpu.HBM((chunks, rows, per_chunk), bf16),
             shape((chunks, 2, per_chunk, features), bf16),
             shape((chunks, rows, per_chunk), bf16), shape((chunks, 1, per_chunk), f32)),
            [vec, fixed(hidden_half), fixed(rows, features), fixed(rows, features),
             pl.BlockSpec((features, per_chunk), lambda j: (0, j)),
             pl.BlockSpec((per_chunk, features), lambda j: (j, 0))],
            8 * rows * features * hidden_half, 1e7, (scale, b1, normed2, cotangent, w1, w2),
            deps=deps, grid=(chunks,),
            out_specs=(part, pl.BlockSpec((1, 2, per_chunk, features), lambda j: (j, 0, 0, 0)), part,
                       pl.BlockSpec((1, 1, per_chunk), lambda j: (j, 0, 0))),
            scratch=[pltpu.VMEM((rows, features), bf16), pltpu.VMEM((1, hidden_half), f32)],
            vmem=VMEM_MLP, transcendentals=2 * rows * hidden_half,
        )

    def grouped(own, par, name):
        flat_shape = (-1, own.shape[-1])
        return GroupSum(own.reshape(flat_shape), par.reshape(flat_shape), axes, name)

    vec = fixed(features)
    h_par, pack_par, gb_par, b1_par = mlp(fc1_par, fc1_bias_par, fc2_par, "mlp_par")
    received = other(pack_par)
    h_own, pack_own, gb_own, b1_own = mlp(fc1_weight, fc1_bias, fc2_weight, "mlp_own", [pack_par])
    group_0 = grouped(pack_own[0], received[0], "g0")
    group_1 = grouped(pack_own[1], received[1], "g1")
    token = group_0.scatter([pack_own])
    token = group_1.scatter([token])

    small = shape((1, features), f32)
    dwo_shape = shape((features, width), bf16)
    (
        grad_middle, ga_own, ga_par, dwo_own, dwo_par, d_gain2, d_bias2, d_attn_scale, d_out_bias,
    ) = staged(
        project_back_kernel, "project_back",
        (ln2_gain, attn_scale, gb_own, gb_par),
        (fc1_weight, fc1_par, middle, patches, cotangent, att_own, att_par, out_weight, out_par),
        (row_f32,), (att_shape, att_shape, dwo_shape, dwo_shape) + (small,) * 4,
        [w1_shape] * 2
        + [row_f32, row_bf16, row_bf16, att_shape, att_shape, w_shape, w_shape, row_f32],
        8 * rows * width * features + 8 * rows * features * per_chunk, VMEM_MLP, deps=(token,),
    )

    pack = shape((4 * features, width), bf16)
    bias_shape = shape((2, width), f32)
    acc_shapes = [shape((ext, PAIR), f32)] * 2
    ext_width = shape((ext, width), bf16)
    back_scratch = head_shapes + share_shapes + [ext_bf16, weight_shape]
    back_scratch += [att_shape, ext_width, ext_width] + acc_shapes
    back_flops = 8 * area * PAIR + 2 * qkv_flops

    def back_first(*refs):
        attend_back_kernel(*refs[:3], None, *refs[3:15], None, None, *refs[15:-1], None, refs[-1])

    def back_second(*refs):
        grad_own_out, pack_ref, bias_ref, grad_halo_ref = refs[13:17]
        attend_back_kernel(
            *refs[:13], pack_ref, bias_ref, refs[-2], grad_own_out, grad_halo_ref, *refs[17:-2],
            refs[-1],
        )

    pack_par, qb_par, partial_total = staged(
        back_first, "attend_back_par", (side, ga_par, dwo_par), (*heads_par, normed1, qkv_par),
        (), (pack, bias_shape, ext_f32), back_scratch, back_flops, VMEM_BACK, deps=(grad_middle,),
    )
    token = group_0.scatter([pack_par])
    pack_received = other(pack_par)

    grad_own, pack_own, qb_own, grad_halo = staged(
        back_second, "attend_back_own", (side, ga_own, dwo_own, partial_total),
        (*heads_own, normed1, qkv_weight),
        (row_f32,), (pack, bias_shape, halo_shape), back_scratch + [row_f32, ext_f32], back_flops,
        VMEM_BACK + 4, deps=(token,),
    )
    halo_back = other(grad_halo)
    group_2 = grouped(pack_own, pack_received, "g2")
    token = pack_own
    if group_0.stage < len(axes):
        token = group_0.scatter([token])
    token = group_1.scatter([token])
    token = group_2.scatter([token])
    while group_0.stage < len(axes):
        token = group_0.scatter([token])
    token = group_0.turn([token])
    while group_1.stage < len(axes):
        token = group_1.scatter([token])
    if group_0.split:
        token = group_0.gather([token])

    grad_patches, d_gain1, d_bias1 = call(
        norm1_back_kernel, "norm1_back", (row_f32, small, small), [SCALARS] + [WHOLE] * 5,
        20 * rows * features, 6e6,
        (side, grad_own, halo_back, patches, ln1_gain, grad_middle), deps=(token,),
        scratch=[pltpu.VMEM((rows, features), f32)],
    )
    vectors = shape((VECTOR_ROWS, features), f32)
    output, mine, theirs = call(
        finish_kernel, "finish", (row_bf16, vectors, vectors), [WHOLE] * 18,
        20 * rows * features, 8e6,
        (h_own, h_par, fc2_weight, fc2_par, middle, cotangent, fc2_bias, mlp_scale,
         d_gain1, d_bias1, d_gain2, d_bias2, d_attn_scale, d_out_bias, qb_own, qb_par,
         b1_own, b1_par),
        deps=(d_gain1,),
    )
    vector_terms = [mine, other(theirs)]

    def add_vectors(deps):
        return call(
            partial(add_kernel, terms=len(vector_terms)), "add_vectors", vectors,
            [WHOLE] * len(vector_terms), 1e5, 2e5, vector_terms, deps=deps,
        )

    token = mine
    pending = [group_1, group_0, group_2]
    vector_axes = list(axes)
    while any(g.stage < len(axes) for g in pending) or vector_axes:
        for group in (group_1, group_2):
            if group.stage < len(axes):
                token = group.scatter([token])
        if vector_axes:
            axis = vector_axes.pop(0)
            total = add_vectors([token])
            vector_terms = [total] + [axis.send(total, s) for s in range(1, axis.length)]
            token = total
        if group_0.split:
            token = group_0.gather([token])
    token = group_1.turn([token])
    token = group_2.turn([token])
    groups = (group_0, group_1, group_2)
    while any(group.split for group in groups):
        for group in groups:
            if group.split:
                token = group.gather([token])
    fast = all(len(group.parts) == 2 for group in groups)
    if fast:
        fc = unpack_fc(group_0, 0, chunks, (), [token], "unpack_0")
        fc = unpack_fc(group_1, 1, chunks, fc, [], "unpack_1")
        grad_fc2_weight, grad_fc1_weight = fc
        token = grad_fc2_weight

    one = shape((features,), f32)
    (
        d_gain1, d_bias1, d_gain2, d_bias2, d_attn_scale, d_out_bias, d_mlp_scale, d_fc2_bias,
        grad_qkv_bias, grad_fc1_bias,
    ) = call(
        partial(unpack_kernel, terms=len(vector_terms), deps=0), "unpack",
        (one,) * 8 + (shape((2, width), f32), shape((hidden_half,), f32)),
        [WHOLE] * len(vector_terms), 1e5, 2e5, vector_terms, deps=(token,),
    )

    if fast:
        grad_qkv_weight, grad_out_weight = unpack_qkv(group_2, [token], "unpack_2")
    else:
        fc_0, fc_1, qkv = [group.join([token]) for group in groups]
        grad_fc2_weight = jnp.concatenate([fc_0[:per_chunk], fc_1[:per_chunk]], axis=0).astype(f32)
        grad_fc1_weight = jnp.concatenate([fc_0[per_chunk:], fc_1[per_chunk:]], axis=0).astype(f32).T
        grad_qkv_weight = qkv[: 3 * features].astype(f32).reshape(3, features, width)
        tail = qkv[3 * features :].astype(f32)
        grad_out_weight = jnp.concatenate(
            [tail[part * width : (part + 1) * width] for part in range(features // width)], axis=1
        )
    return (
        output,
        grad_patches,
        d_gain1,
        d_bias1,
        grad_qkv_weight,
        grad_qkv_bias,
        grad_out_weight,
        d_out_bias,
        d_attn_scale,
        d_gain2,
        d_bias2,
        grad_fc1_weight,
        grad_fc1_bias,
        grad_fc2_weight,
        d_fc2_bias,
        d_mlp_scale,
    )


def solution(mesh):
    in_specs = (
        P(("wide", "narrow"), None),
        P("wide", None),
        P(),
        P(),
        P(None, None, "narrow"),
        P(None, "narrow"),
        P("narrow", None),
        P(),
        P(),
        P(),
        P(),
        P(None, "narrow"),
        P("narrow"),
        P("narrow", None),
        P(),
        P(),
        P(("wide", "narrow"), None),
    )
    out_specs = (
        P(("wide", "narrow"), None),
        P(("wide", "narrow"), None),
        P(),
        P(),
        P(None, None, "narrow"),
        P(None, "narrow"),
        P("narrow", None),
        P(),
        P(),
        P(),
        P(),
        P(None, "narrow"),
        P("narrow"),
        P("narrow", None),
        P(),
        P(),
    )
    return jax.shard_map(
        on_device, mesh=mesh, in_specs=in_specs, out_specs=out_specs, check_vma=False
    )
```
